32 devices in a mesh: rep: 2 (over x), seq: 8 (over z, y), chan: 2 (over core).
Axes of the slice: x: 2, y: 2, z: 4, core: 2. Of those that a mesh axis runs over, the one named last changes fastest.
Arguments:
- inputs: float32 [32768, 256], P(('rep', 'seq'), 'chan'), parts along dimension 0, may hold values from -6 to 6
- gate_in: float32 [32768, 256], P(('rep', 'seq'), 'chan'), parts along dimension 0, may hold values from -6 to 6
- out_grad: float32 [32768, 256], P(('rep', 'seq'), 'chan'), parts along dimension 0, may hold values from -6 to 6
- w_first: float32 [1024, 1024], P(('seq', 'chan')), may hold values from -0.1875 to 0.1875
- w_second: float32 [16, 16], replicated, may hold values from -1.5 to 1.5
- w_out: float32 [256, 256], replicated, may hold values from -0.375 to 0.375
Outputs:
- input_grad: float32 [32768, 256], P(('rep', 'seq'), 'chan'), parts along dimension 0
- gate_grad: float32 [32768, 256], P(('rep', 'seq'), 'chan'), parts along dimension 0
- first_grad: float32 [2048, 1024], P(('rep', 'seq', 'chan')), parts along dimension 0
- second_grad: float32 [32, 16], P('rep'), parts along dimension 0
The draws below stay inside these ranges and needn't reach their ends.
There are 2 independent parts, one for each index of `rep`. The reference program is written for one: setup_inputs(seed, part) draws one part's arguments, and reference() takes and returns one part's arrays. A program takes and returns all parts, laid end to end along the dimension named above; an argument that names none is the same for every part. Nothing has to cross between parts.
All inputs are finite; a program needn't handle non-finite values.
Results may differ from the reference program's by a relative error of at most 0.00013.
Values sent between devices are 32-bit elements; how exact they have to be, the bound alone decides.
No kernel may reach another device: no remote copies, remote signals or barrier semaphores. Data moves between devices by JAX's collectives and lax.ppermute only.
A program may use at most 64 MiB of HBM per device.

```python
import math
import jax
import jax.numpy as jnp
from jax import lax

B = 1024
C = 256
NBLK = 16
LEN = 16384


def shard_levels(rng, dims, pieces, smallest, largest):
    def one(dim, shards_of):
        draws = jax.random.uniform(jax.random.fold_in(jax.random.fold_in(rng, 6), dim), (shards_of,), jnp.float32, smallest / len(pieces), largest / len(pieces))
        return jnp.repeat(jnp.exp(draws), dims[dim] // shards_of).reshape((-1,) + (1,) * (len(dims) - dim - 1))

    loudness = one(*pieces[0])
    for cut in pieces[1:]:
        loudness = loudness * one(*cut)
    return loudness


def noise(key, extent, deviation, reach, cuts=(), kind=jnp.bfloat16):
    drawn = jax.random.normal(key, extent, jnp.float32) * deviation
    if len(cuts) > 0:
        drawn = shard_levels(key, extent, cuts, -0.22, 0.18) * drawn
    return jnp.clip(drawn, min=-reach, max=reach).astype(kind)


def setup_inputs(seed: int = 0, part: int = 0) -> dict:
    seeds = jax.random.split(jax.random.key(seed), 7)
    own_keys = jax.random.split(jax.random.fold_in(seeds[6], part), 7)
    inputs = noise(own_keys[0], (LEN, C), 1.0, 6.0, ((0, 8), (1, 2)), jnp.float32)
    gate_in = noise(own_keys[1], (LEN, C), 1.0, 6.0, ((0, 8), (1, 2)), jnp.float32)
    out_grad = noise(own_keys[2], (LEN, C), 1.0, 6.0, ((0, 8), (1, 2)), jnp.float32)
    w_first = noise(seeds[3], (B, B), B ** -0.5, 0.1875, ((0, 16),), jnp.float32)
    w_second = noise(seeds[4], (NBLK, NBLK), NBLK ** -0.5, 1.5, (), jnp.float32)
    w_out = noise(seeds[5], (C, C), C ** -0.5, 0.375, (), jnp.float32)
    return {"inputs": inputs, "gate_in": gate_in, "out_grad": out_grad, "w_first": w_first, "w_second": w_second, "w_out": w_out}


def reference(inputs, gate_in, out_grad, w_first, w_second, w_out):
    highest = lax.Precision.HIGHEST
    blocks = inputs.reshape(NBLK, B, C)
    gate_vals = gate_in.reshape(NBLK, B, C)
    tile_vals = jnp.einsum('kj,ijc->ikc', w_first, blocks, precision=highest)
    mixed_vals = jnp.einsum('mi,ikc->mkc', w_second, tile_vals, precision=highest)
    hidden_grad = jnp.dot(out_grad, w_out.T, precision=highest).reshape(NBLK, B, C)
    squash = jax.nn.sigmoid(gate_vals)
    mixed_grad = hidden_grad * gate_vals * squash
    gate_grad = hidden_grad * mixed_vals * squash * (1.0 + gate_vals * (1.0 - squash))
    tile_grad = jnp.einsum('mi,mkc->ikc', w_second, mixed_grad, precision=highest)
    second_grad = jnp.einsum('mkc,ikc->mi', mixed_grad, tile_vals, precision=highest) * (1.0 / math.sqrt(B * C))
    input_grad = jnp.einsum('kj,ikc->ijc', w_first, tile_grad, precision=highest).reshape(LEN, C)
    first_grad = jnp.einsum('ikc,ijc->kj', tile_grad, blocks, precision=highest) * (1.0 / math.sqrt(NBLK * C))
    return (input_grad, gate_grad.reshape(LEN, C), first_grad, second_grad)
```

```python
import functools
import math

import jax
import jax.numpy as jnp
from jax import lax
from jax.experimental import pallas as pl
from jax.experimental.pallas import tpu as pltpu
from jax.sharding import PartitionSpec as P

F32 = jnp.float32
BF16 = jnp.bfloat16
NN = (((1,), (0,)), ((), ()))
NT = (((1,), (1,)), ((), ()))
TN = (((0,), (0,)), ((), ()))
VMEM_LIMIT = 48 * 1024 * 1024


def split(x):
    hi = x.astype(BF16)
    return hi, (x - hi.astype(F32)).astype(BF16)


def dot3(a, b, dims):
    (ah, al), (bh, bl) = a, b

    def d(u, v):
        return lax.dot_general(u, v, dims, preferred_element_type=F32)

    return d(ah, bh) + (d(ah, bl) + d(al, bh))


def params():
    return pltpu.CompilerParams(vmem_limit_bytes=VMEM_LIMIT)


def cost(flops, size):
    return pl.CostEstimate(flops=flops, bytes_accessed=size, transcendentals=0)


def gate_kernel(own_ref, other_ref, gate_ref, w_ref, grad_ref, factor_ref):
    cot = jnp.concatenate([own_ref[...], other_ref[...]], axis=1)
    hidden = dot3(split(cot), split(w_ref[...]), NT)
    g = gate_ref[...]
    s = jax.nn.sigmoid(g)
    hs = hidden * s
    grad_ref[...] = hs * g
    factor_ref[...] = hs * (1.0 + g * (1.0 - s))


def gate_call(own, other, gate, w):
    rows, width = own.shape
    tile = rows // 4
    row = pl.BlockSpec((tile, width), lambda i: (i, 0))
    shape = jax.ShapeDtypeStruct(own.shape, F32)
    return pl.pallas_call(
        gate_kernel,
        grid=(4,),
        in_specs=[row, row, row, pl.BlockSpec(w.shape, lambda i: (0, 0))],
        out_specs=[row, row],
        out_shape=[shape, shape],
        compiler_params=params(),
        cost_estimate=cost(6 * rows * width * 2 * width, 5 * 4 * rows * width),
        name="gate",
    )(own, other, gate, w)


def grouped(ref, group):
    n, span, width = ref.shape
    return jnp.concatenate(
        [ref[:, g * group : (g + 1) * group, :].reshape(n * group, width) for g in range(span // group)], axis=1
    )


def scatter_groups(ref, group, val):
    n, span, width = ref.shape
    for g in range(span // group):
        ref[:, g * group : (g + 1) * group, :] = val[:, g * width : (g + 1) * width].reshape(n, group, width)


def mix_kernel(group, k_ref, x_ref, o_ref):
    x = grouped(x_ref, group)
    scatter_groups(o_ref, group, dot3(split(k_ref[...]), split(x), NN))


def mix_second_kernel(group, scale, k_ref, u_ref, b_ref, o_ref, s_ref, acc):
    step = pl.program_id(0)
    u = split(grouped(u_ref, group))
    b = split(grouped(b_ref, group))
    scatter_groups(o_ref, group, dot3(split(k_ref[...]), u, NN))

    @pl.when(step == 0)
    def _():
        acc[...] = jnp.zeros_like(acc)

    acc[...] += dot3(u, b, NT)

    @pl.when(step == pl.num_programs(0) - 1)
    def _():
        size = acc.shape[0]
        n = size // group
        r = lax.broadcasted_iota(jnp.int32, (size, size), 0)
        c = lax.broadcasted_iota(jnp.int32, (size, size), 1)
        diag = jnp.where(lax.rem(r, group) == lax.rem(c, group), acc[...], 0.0)
        rows = jnp.sum(diag.reshape(n, group, size), axis=1)
        pick_r = lax.broadcasted_iota(jnp.int32, (size, n), 0)
        pick_c = lax.broadcasted_iota(jnp.int32, (size, n), 1)
        pick = (lax.div(pick_r, group) == pick_c).astype(F32)
        s_ref[...] = jnp.dot(rows, pick, precision=lax.Precision.HIGHEST, preferred_element_type=F32) * scale


def mix_call(kron, x, group):
    n, width, chan = x.shape
    span = min(width, 2 * group)
    block = pl.BlockSpec((n, span, chan), lambda i: (0, i, 0))
    size = kron.shape[0]
    return pl.pallas_call(
        functools.partial(mix_kernel, group),
        grid=(width // span,),
        in_specs=[pl.BlockSpec(kron.shape, lambda i: (0, 0)), block],
        out_specs=block,
        out_shape=jax.ShapeDtypeStruct(x.shape, F32),
        compiler_params=params(),
        cost_estimate=cost(6 * size * n * width * chan, 8 * n * width * chan),
        name="mix",
    )(kron, x)


def mix_second_call(kron, u, b, group, scale):
    n, width, chan = u.shape
    span = min(width, 2 * group)
    block = pl.BlockSpec((n, span, chan), lambda i: (0, i, 0))
    size = kron.shape[0]
    return pl.pallas_call(
        functools.partial(mix_second_kernel, group, scale),
        grid=(width // span,),
        in_specs=[pl.BlockSpec(kron.shape, lambda i: (0, 0)), block, block],
        out_specs=[block, pl.BlockSpec((n, n), lambda i: (0, 0))],
        out_shape=[jax.ShapeDtypeStruct(u.shape, F32), jax.ShapeDtypeStruct((n, n), F32)],
        scratch_shapes=[pltpu.VMEM((size, size), F32)],
        compiler_params=params(),
        cost_estimate=cost(12 * size * n * width * chan, 12 * n * width * chan),
        name="mix_second",
    )(kron, u, b)


def place_kernel(offsets, s_ref, h_ref, *refs):
    pieces = refs[: 2 * len(offsets)]
    hi_ref, lo_ref, whole, sem = refs[2 * len(offsets) :]
    unit = pieces[0].shape[1]
    copies = []
    for side in range(2):
        for piece, rels in zip(pieces[side * len(offsets) :], offsets):
            for u, rel in enumerate(rels):
                place = 2 * lax.bitwise_xor(s_ref[0], rel) + lax.bitwise_xor(h_ref[0], side)
                start = pl.multiple_of(place * unit, unit)
                copies.append(
                    pltpu.make_async_copy(piece.at[u], whole.at[pl.ds(start, unit)], sem.at[len(copies)])
                )
    for c in copies:
        c.start()
    for c in copies:
        c.wait()
    rows = whole.shape[0]
    tile = 256
    for t in range(rows // tile):
        hi, lo = split(whole[t * tile : (t + 1) * tile, :])
        hi_ref[t * tile : (t + 1) * tile, :] = hi
        lo_ref[t * tile : (t + 1) * tile, :] = lo


def place_call(seq_id, chan_id, pieces, offsets, rows, columns):
    shape = jax.ShapeDtypeStruct((rows, columns), BF16)
    smem = pl.BlockSpec(memory_space=pltpu.SMEM)
    vmem = pl.BlockSpec(memory_space=pltpu.VMEM)
    return pl.pallas_call(
        functools.partial(place_kernel, offsets),
        in_specs=[smem, smem] + [pl.BlockSpec(memory_space=pl.ANY)] * len(pieces),
        out_specs=[vmem, vmem],
        out_shape=[shape, shape],
        scratch_shapes=[pltpu.VMEM((rows, columns), F32), pltpu.SemaphoreType.DMA((2 * sum(map(len, offsets)),))],
        compiler_params=params(),
        cost_estimate=cost(rows * columns, 8 * rows * columns),
        name="place",
    )(seq_id, chan_id, *pieces)


def up_kernel(hi_ref, lo_ref, g_ref, o_ref, gh, gl):
    @pl.when(pl.program_id(0) == 0)
    def _():
        both = jnp.concatenate([g_ref[m] for m in range(g_ref.shape[0])], axis=1)
        gh[...], gl[...] = split(both)

    res = dot3((hi_ref[...], lo_ref[...]), (gh[...], gl[...]), TN)
    slices, blocks, width, chan = o_ref.shape
    for t in range(slices):
        for m in range(blocks):
            o_ref[t, m] = res[t * width : (t + 1) * width, m * chan : (m + 1) * chan]


def up_call(hi, lo, grad, slices):
    blocks, rows, chan = grad.shape
    tile = 256
    width = rows // slices
    per = tile // width
    wspec = pl.BlockSpec((rows, tile), lambda i: (0, i))
    return pl.pallas_call(
        up_kernel,
        grid=(rows // tile,),
        in_specs=[wspec, wspec, pl.BlockSpec(grad.shape, lambda i: (0, 0, 0))],
        out_specs=pl.BlockSpec((per, blocks, width, chan), lambda i: (i, 0, 0, 0)),
        out_shape=jax.ShapeDtypeStruct((slices, blocks, width, chan), F32),
        scratch_shapes=[pltpu.VMEM((rows, blocks * chan), BF16)] * 2,
        compiler_params=params(),
        cost_estimate=cost(6 * rows * rows * blocks * chan, 4 * rows * rows + 8 * rows * blocks * chan),
        name="up",
    )(hi, lo, grad)


def join(ref):
    slices, blocks = ref.shape[0], ref.shape[1]
    return jnp.concatenate(
        [jnp.concatenate([ref[t, m] for m in range(blocks)], axis=1) for t in range(slices)], axis=0
    )


def mixed_kernel(hi_ref, lo_ref, v_ref, f_ref, o_ref, vh, vl):
    @pl.when(pl.program_id(0) == 0)
    def _():
        vh[...], vl[...] = split(join(v_ref))

    res = dot3((hi_ref[...], lo_ref[...]), (vh[...], vl[...]), NN)
    chan = o_ref.shape[2]
    for m in range(o_ref.shape[0]):
        o_ref[m] = res[:, m * chan : (m + 1) * chan] * f_ref[m]


def mixed_call(hi, lo, v, factor):
    blocks, rows, chan = factor.shape
    tile = 256
    wspec = pl.BlockSpec((tile, rows), lambda i: (i, 0))
    ospec = pl.BlockSpec((blocks, tile, chan), lambda i: (0, i, 0))
    return pl.pallas_call(
        mixed_kernel,
        grid=(rows // tile,),
        in_specs=[wspec, wspec, pl.BlockSpec(v.shape, lambda i: (0, 0, 0, 0)), ospec],
        out_specs=ospec,
        out_shape=jax.ShapeDtypeStruct(factor.shape, F32),
        scratch_shapes=[pltpu.VMEM((rows, blocks * chan), BF16)] * 2,
        compiler_params=params(),
        cost_estimate=cost(6 * rows * rows * blocks * chan, 4 * rows * rows + 12 * rows * blocks * chan),
        name="mixed",
    )(hi, lo, v, factor)


def flip_bits(q, bits):
    r = 0
    for b in range(bits):
        r |= ((q >> b) & 1) << (bits - 1 - b)
    return r


def first_kernel(bits, s_ref, ga_ref, gb_ref, va_ref, vb_ref, keep_ref, send_ref, lh, ll):
    count, unit = ga_ref.shape[1], ga_ref.shape[2]
    blocks = ga_ref.shape[0]

    @pl.when(pl.program_id(0) == 0)
    def _():
        for q in range(count):
            src = lax.bitwise_xor(s_ref[0], flip_bits(q, bits))
            row = jnp.concatenate([r[m, src] for m in range(blocks) for r in (ga_ref, gb_ref)], axis=1)
            lh[q * unit : (q + 1) * unit, :], ll[q * unit : (q + 1) * unit, :] = split(row)

    v = jnp.concatenate(
        [
            jnp.concatenate([r[t, m] for m in range(blocks) for r in (va_ref, vb_ref)], axis=1)
            for t in range(va_ref.shape[0])
        ],
        axis=0,
    )
    res = dot3((lh[...], ll[...]), split(v), NT)
    half = count // 2
    for q in range(half):
        keep_ref[q] = res[q * unit : (q + 1) * unit, :]
        send_ref[q] = res[(half + q) * unit : (half + q + 1) * unit, :]


def first_call(seq_id, grad_own, grad_other, v_own, v_other):
    blocks, count, unit, chan = grad_own.shape
    slices, _, width, _ = v_own.shape
    rows = slices * width
    tile = 256
    per = tile // width
    bits = count.bit_length() - 1
    gspec = pl.BlockSpec(grad_own.shape, lambda i: (0, 0, 0, 0))
    vspec = pl.BlockSpec((per, blocks, width, chan), lambda i: (i, 0, 0, 0))
    ospec = pl.BlockSpec((count // 2, unit, tile), lambda i: (0, 0, i))
    shape = jax.ShapeDtypeStruct((count // 2, unit, rows), F32)
    depth = 2 * blocks * chan
    return pl.pallas_call(
        functools.partial(first_kernel, bits),
        grid=(rows // tile,),
        in_specs=[pl.BlockSpec(memory_space=pltpu.SMEM), gspec, gspec, vspec, vspec],
        out_specs=[ospec, ospec],
        out_shape=[shape, shape],
        scratch_shapes=[pltpu.VMEM((count * unit, depth), BF16)] * 2,
        compiler_params=params(),
        cost_estimate=cost(6 * rows * count * unit * depth, 4 * (rows * count * unit + 2 * rows * depth)),
        name="first",
    )(seq_id, grad_own, grad_other, v_own, v_other)


def body(seq_count, inputs, gate_in, out_grad, w_first, w_second, w_out):
    total = w_second.shape[0]
    own = total // seq_count
    rows = inputs.shape[0] // own
    chan = inputs.shape[1]
    width = rows // seq_count
    unit, columns = w_first.shape
    bits = seq_count.bit_length() - 1
    s = lax.axis_index("seq").astype(jnp.int32)
    h = lax.axis_index("chan").astype(jnp.int32)
    seq_id, chan_id = s.reshape(1), h.reshape(1)
    group = 16 if total * 16 <= 256 else 8

    def swap_core(x):
        return lax.ppermute(x, "chan", [(0, 1), (1, 0)])

    def swap_seq(x, bit):
        return lax.ppermute(x, "seq", [(i, i ^ bit) for i in range(seq_count)])

    def exchange(x):
        return lax.all_to_all(x, "seq", split_axis=0, concat_axis=0, tiled=True)

    other_cot = swap_core(out_grad)
    eye = jnp.eye(group, dtype=F32)
    kron = (w_second[:, None, :, None] * eye[None, :, None, :]).reshape(total * group, total * group)
    kron_t = (w_second.T[:, None, :, None] * eye[None, :, None, :]).reshape(total * group, total * group)

    sliced = inputs.reshape(own, seq_count, width, chan).transpose(1, 0, 2, 3)
    block_cols = exchange(sliced).reshape(total, width, chan)
    v_cols = mix_call(kron, block_cols, group)
    v = exchange(v_cols.reshape(seq_count, own, width, chan))

    pieces, offsets = [w_first.reshape(1, unit, columns)], [(0,)]
    for b in reversed(range(bits)):
        held = pieces[0] if len(pieces) == 1 else jnp.concatenate(pieces, axis=0)
        pieces.append(swap_seq(held, 1 << b))
        offsets.append(tuple(r ^ (1 << b) for r in sum(offsets, ())))

    own_rows = lax.dynamic_slice_in_dim(w_out, h * chan, chan, 0)
    w_cat = jnp.concatenate(
        [
            lax.dynamic_slice_in_dim(own_rows, h * chan, chan, 1),
            lax.dynamic_slice_in_dim(own_rows, (1 - h) * chan, chan, 1),
        ],
        axis=1,
    )
    grad, factor = gate_call(out_grad, other_cot, gate_in, w_cat)
    by_core = grad.reshape(own, seq_count, 2, unit, chan)
    grad_own = lax.dynamic_index_in_dim(by_core, h, 2, keepdims=False)
    grad_other = swap_core(lax.dynamic_index_in_dim(by_core, 1 - h, 2, keepdims=False))

    far = [swap_core(p) for p in pieces]
    hi, lo = place_call(seq_id, chan_id, pieces + far, tuple(offsets), rows, columns)
    u = up_call(hi, lo, grad.reshape(own, rows, chan), seq_count)
    u_cols = exchange(u).reshape(total, width, chan)
    in_cols, second = mix_second_call(kron_t, u_cols, block_cols, group, 1.0 / math.sqrt(rows * 2 * chan))
    back = exchange(in_cols.reshape(seq_count, own, width, chan))
    input_grad = back.transpose(1, 0, 2, 3).reshape(inputs.shape)
    second = second + swap_core(second)
    for b in range(bits):
        second = second + swap_seq(second, 1 << b)

    gate_grad = mixed_call(hi, lo, v, factor.reshape(own, rows, chan)).reshape(inputs.shape)
    keep, send = first_call(seq_id, grad_own, grad_other, v, swap_core(v))
    for b in range(bits):
        keep = keep + swap_seq(send, 1 << b)
        if b + 1 < bits:
            half = keep.shape[0] // 2
            keep, send = keep[:half], keep[half:]
    first_grad = keep.reshape(unit, columns) * (1.0 / math.sqrt(total * 2 * chan))
    return input_grad, gate_grad, first_grad, second


def solution(mesh):
    return jax.shard_map(
        functools.partial(body, mesh.shape["seq"]),
        mesh=mesh,
        in_specs=(
            P(("rep", "seq"), "chan"),
            P(("rep", "seq"), "chan"),
            P(("rep", "seq"), "chan"),
            P(("seq", "chan"), None),
            P(),
            P(),
        ),
        out_specs=(
            P(("rep", "seq"), "chan"),
            P(("rep", "seq"), "chan"),
            P(("rep", "seq", "chan"), None),
            P("rep", None),
        ),
        check_vma=False,
    )
```

```python
import functools
import math

import jax
import jax.numpy as jnp
from jax import lax
from jax.experimental import pallas as pl
from jax.experimental.pallas import tpu as pltpu
from jax.sharding import PartitionSpec as P

F32 = jnp.float32
BF16 = jnp.bfloat16
NN = (((1,), (0,)), ((), ()))
NT = (((1,), (1,)), ((), ()))
TN = (((0,), (0,)), ((), ()))
VMEM_LIMIT = 16 * 1024 * 1024


def split(x):
    hi = x.astype(BF16)
    return hi, (x - hi.astype(F32)).astype(BF16)


def dot3(a, b, dims):
    (ah, al), (bh, bl) = a, b

    def d(u, v):
        return lax.dot_general(u, v, dims, preferred_element_type=F32)

    return d(ah, bh) + (d(ah, bl) + d(al, bh))


def params():
    return pltpu.CompilerParams(vmem_limit_bytes=VMEM_LIMIT)


def cost(flops, size):
    return pl.CostEstimate(flops=flops, bytes_accessed=size, transcendentals=0)


def gate_kernel(ids_ref, own_ref, other_ref, gate_ref, w_ref, grad_ref, factor_ref, mine_ref, send_ref):
    cot = jnp.concatenate([own_ref[...], other_ref[...]], axis=1)
    hidden = dot3(split(cot), split(w_ref[...]), NT)
    g = gate_ref[...]
    s = jax.nn.sigmoid(g)
    hs = hidden * s
    grad = hs * g
    grad_ref[...] = grad
    _, count, unit, width = mine_ref.shape
    pairs = grad.reshape(count, 2, unit, width)
    low = ids_ref[1] == 0
    mine_ref[0] = jnp.where(low, pairs[:, 0], pairs[:, 1])
    send_ref[0] = jnp.where(low, pairs[:, 1], pairs[:, 0])
    factor_ref[...] = hs * (1.0 + g * (1.0 - s))


def gate_call(ids, own, other, gate, w, blocks, unit):
    rows, width = own.shape
    per = 2
    tile = rows // blocks // per
    count = tile // (2 * unit)
    row = pl.BlockSpec((tile, width), lambda i: (i, 0))
    part = pl.BlockSpec((1, count, unit, width), lambda i: (i // per, i % per, 0, 0))
    shape = jax.ShapeDtypeStruct(own.shape, F32)
    part_shape = jax.ShapeDtypeStruct((blocks, per * count, unit, width), F32)
    return pl.pallas_call(
        gate_kernel,
        grid=(blocks * per,),
        in_specs=[
            pl.BlockSpec(memory_space=pltpu.SMEM),
            row,
            row,
            row,
            pl.BlockSpec(w.shape, lambda i: (0, 0)),
        ],
        out_specs=[row, row, part, part],
        out_shape=[shape, shape, part_shape, part_shape],
        compiler_params=params(),
        cost_estimate=cost(6 * rows * width * 2 * width, 6 * 4 * rows * width),
        name="gate",
    )(ids, own, other, gate, w)


def grouped(ref, group):
    n, span, width = ref.shape
    return jnp.concatenate(
        [ref[:, g * group : (g + 1) * group, :].reshape(n * group, width) for g in range(span // group)], axis=1
    )


def scatter_groups(ref, group, val):
    n, span, width = ref.shape
    for g in range(span // group):
        ref[:, g * group : (g + 1) * group, :] = val[:, g * width : (g + 1) * width].reshape(n, group, width)


def spread(w, group):
    n = w.shape[0]
    size = n * group
    pick = (
        lax.div(lax.broadcasted_iota(jnp.int32, (size, n), 0), group)
        == lax.broadcasted_iota(jnp.int32, (size, n), 1)
    ).astype(F32)

    def d(a, b, dims):
        return lax.dot_general(a, b, dims, precision=lax.Precision.HIGHEST, preferred_element_type=F32)

    full = d(d(pick, w, NN), pick, NT)
    r = lax.broadcasted_iota(jnp.int32, (size, size), 0)
    c = lax.broadcasted_iota(jnp.int32, (size, size), 1)
    return jnp.where(lax.rem(r, group) == lax.rem(c, group), full, 0.0)


def spread_kernel(group, w_ref, kh, kl, th, tl):
    w = w_ref[...]
    kh[...], kl[...] = split(spread(w, group))
    th[...], tl[...] = split(spread(w.T, group))


def spread_call(w, group):
    size = w.shape[0] * group
    return pl.pallas_call(
        functools.partial(spread_kernel, group),
        out_shape=[jax.ShapeDtypeStruct((size, size), BF16)] * 4,
        compiler_params=params(),
        cost_estimate=cost(8 * size * size * w.shape[0], 8 * size * size),
        name="spread",
    )(w)


def spans(width, group):
    step = min(width, 2 * group)
    return [(a, step) for a in range(0, width, step)]


def mix_kernel(group, kh, kl, x_ref, o_ref):
    k = kh[...], kl[...]
    for a, step in spans(x_ref.shape[1], group):
        x = grouped(x_ref.at[:, a : a + step], group)
        scatter_groups(o_ref.at[:, a : a + step], group, dot3(k, split(x), NN))


def mix_second_kernel(group, scale, own, kh, kl, u_ref, b_ref, o_ref, acc):
    k = kh[...], kl[...]
    n, width, _ = u_ref.shape
    for a, step in spans(width, group):
        u = split(grouped(u_ref.at[:, a : a + step], group))
        b = split(grouped(b_ref.at[:, a : a + step], group))
        scatter_groups(o_ref.at[:, a : a + step], group, dot3(k, u, NN))
        term = dot3(u, b, NT)
        acc[...] = term if a == 0 else acc[...] + term
    size = n * group
    r = lax.broadcasted_iota(jnp.int32, (size, size), 0)
    c = lax.broadcasted_iota(jnp.int32, (size, size), 1)
    diag = jnp.where(lax.rem(r, group) == lax.rem(c, group), acc[...], 0.0)
    rows = jnp.sum(diag.reshape(n, group, size), axis=1)
    lanes = o_ref.shape[2]
    pick = (
        lax.div(lax.broadcasted_iota(jnp.int32, (size, lanes), 0), group)
        == lax.broadcasted_iota(jnp.int32, (size, lanes), 1)
    ).astype(F32)
    second = scale * jnp.dot(rows, pick, precision=lax.Precision.HIGHEST, preferred_element_type=F32)
    part = n // own
    for m in range(n):
        start = (m % own) * part
        o_ref[m, width:, :] = second[start : start + part, :]


def mix_call(k, x, group):
    n, width, chan = x.shape
    return pl.pallas_call(
        functools.partial(mix_kernel, group),
        out_shape=jax.ShapeDtypeStruct(x.shape, F32),
        compiler_params=params(),
        cost_estimate=cost(6 * group * n * n * width * chan, 8 * n * width * chan),
        name="mix",
    )(*k, x)


def mix_second_call(k, u, b, group, own, scale):
    n, width, chan = u.shape
    size = n * group
    return pl.pallas_call(
        functools.partial(mix_second_kernel, group, scale, own),
        out_shape=jax.ShapeDtypeStruct((n, width + n // own, chan), F32),
        scratch_shapes=[pltpu.VMEM((size, size), F32)],
        compiler_params=params(),
        cost_estimate=cost(12 * size * n * width * chan, 12 * n * width * chan),
        name="mix_second",
    )(*k, u, b)


def place_kernel(offsets, ids_ref, *refs):
    pieces = refs[: len(offsets)]
    hi_ref, lo_ref, whole, sem = refs[len(offsets) :]
    half = pieces[0].shape[1]
    copies = []
    for piece, rels in zip(pieces, offsets):
        for u, (rel, side, flip) in enumerate(rels):
            place = 2 * lax.bitwise_xor(ids_ref[0], rel) + lax.bitwise_xor(ids_ref[1], side)
            place = 2 * place + lax.bitwise_xor(ids_ref[2], flip)
            start = pl.multiple_of(place * half, half)
            copies.append(pltpu.make_async_copy(piece.at[u], whole.at[pl.ds(start, half)], sem.at[len(copies)]))
    for c in copies:
        c.start()
    for c in copies:
        c.wait()
    rows = whole.shape[0]
    tile = 256
    for t in range(rows // tile):
        hi, lo = split(whole[t * tile : (t + 1) * tile, :])
        hi_ref[t * tile : (t + 1) * tile, :] = hi
        lo_ref[t * tile : (t + 1) * tile, :] = lo


def place_call(ids, pieces, offsets, rows, columns):
    shape = jax.ShapeDtypeStruct((rows, columns), BF16)
    vmem = pl.BlockSpec(memory_space=pltpu.VMEM)
    return pl.pallas_call(
        functools.partial(place_kernel, offsets),
        in_specs=[pl.BlockSpec(memory_space=pltpu.SMEM)] + [pl.BlockSpec(memory_space=pltpu.HBM)] * len(pieces),
        out_specs=[vmem, vmem],
        out_shape=[shape, shape],
        scratch_shapes=[pltpu.VMEM((rows, columns), F32), pltpu.SemaphoreType.DMA((sum(map(len, offsets)),))],
        compiler_params=params(),
        cost_estimate=cost(rows * columns, 8 * rows * columns),
        name="place",
    )(ids, *pieces)


def up_kernel(hi_ref, lo_ref, g_ref, o_ref, gh, gl):
    @pl.when(pl.program_id(0) == 0)
    def _():
        both = jnp.concatenate([g_ref[m] for m in range(g_ref.shape[0])], axis=1)
        gh[...], gl[...] = split(both)

    res = dot3((hi_ref[...], lo_ref[...]), (gh[...], gl[...]), TN)
    slices, blocks, width, chan = o_ref.shape
    for t in range(slices):
        for m in range(blocks):
            o_ref[t, m] = res[t * width : (t + 1) * width, m * chan : (m + 1) * chan]


def up_call(hi, lo, grad, slices):
    blocks, rows, chan = grad.shape
    tile = 256
    width = rows // slices
    per = tile // width
    wspec = pl.BlockSpec((rows, tile), lambda i: (0, i))
    return pl.pallas_call(
        up_kernel,
        grid=(rows // tile,),
        in_specs=[wspec, wspec, pl.BlockSpec(grad.shape, lambda i: (0, 0, 0))],
        out_specs=pl.BlockSpec((per, blocks, width, chan), lambda i: (i, 0, 0, 0)),
        out_shape=jax.ShapeDtypeStruct((slices, blocks, width, chan), F32),
        scratch_shapes=[pltpu.VMEM((rows, blocks * chan), BF16)] * 2,
        compiler_params=params(),
        cost_estimate=cost(6 * rows * rows * blocks * chan, 4 * rows * rows + 8 * rows * blocks * chan),
        name="up",
    )(hi, lo, grad)


def join(ref):
    slices, blocks = ref.shape[0], ref.shape[1]
    return jnp.concatenate(
        [jnp.concatenate([ref[t, m] for m in range(blocks)], axis=1) for t in range(slices)], axis=0
    )


def mixed_kernel(hi_ref, lo_ref, v_ref, f_ref, o_ref, vh, vl):
    @pl.when(pl.program_id(0) == 0)
    def _():
        vh[...], vl[...] = split(join(v_ref))

    res = dot3((hi_ref[...], lo_ref[...]), (vh[...], vl[...]), NN)
    chan = o_ref.shape[2]
    for m in range(o_ref.shape[0]):
        o_ref[m] = res[:, m * chan : (m + 1) * chan] * f_ref[m]


def mixed_call(hi, lo, v, factor):
    blocks, rows, chan = factor.shape
    tile = 256
    wspec = pl.BlockSpec((tile, rows), lambda i: (i, 0))
    ospec = pl.BlockSpec((blocks, tile, chan), lambda i: (0, i, 0))
    return pl.pallas_call(
        mixed_kernel,
        grid=(rows // tile,),
        in_specs=[wspec, wspec, pl.BlockSpec(v.shape, lambda i: (0, 0, 0, 0)), ospec],
        out_specs=ospec,
        out_shape=jax.ShapeDtypeStruct(factor.shape, F32),
        scratch_shapes=[pltpu.VMEM((rows, blocks * chan), BF16)] * 2,
        compiler_params=params(),
        cost_estimate=cost(6 * rows * rows * blocks * chan, 4 * rows * rows + 12 * rows * blocks * chan),
        name="mixed",
    )(hi, lo, v, factor)


def flip_bits(q, bits):
    r = 0
    for b in range(bits):
        r |= ((q >> b) & 1) << (bits - 1 - b)
    return r


def first_kernel(bits, ids_ref, ga_ref, gb_ref, va_ref, vb_ref, ka_ref, sa_ref, kb_ref, sb_ref, lh, ll):
    count, unit = ga_ref.shape[1], ga_ref.shape[2]
    blocks = ga_ref.shape[0]

    @pl.when(pl.program_id(0) == 0)
    def _():
        for q in range(count):
            src = lax.bitwise_xor(ids_ref[0], flip_bits(q, bits))
            row = jnp.concatenate([r[m, src] for m in range(blocks) for r in (ga_ref, gb_ref)], axis=1)
            lh[q * unit : (q + 1) * unit, :], ll[q * unit : (q + 1) * unit, :] = split(row)

    v = jnp.concatenate(
        [
            jnp.concatenate([r[t, m] for m in range(blocks) for r in (va_ref, vb_ref)], axis=1)
            for t in range(va_ref.shape[0])
        ],
        axis=0,
    )
    res = dot3((lh[...], ll[...]), split(v), NT)
    quarter, half = count // 4, unit // 2
    for q in range(count):
        r0, r1, rest = q // (2 * quarter), (q // quarter) % 2, q % quarter
        (sa_ref if r0 else ka_ref)[r1 * quarter + rest] = res[q * unit : q * unit + half, :]
        (sb_ref if r1 else kb_ref)[r0 * quarter + rest] = res[q * unit + half : (q + 1) * unit, :]


def first_call(ids, grad_own, grad_other, v_own, v_other):
    blocks, count, unit, chan = grad_own.shape
    slices, _, width, _ = v_own.shape
    rows = slices * width
    tile = 256
    per = tile // width
    bits = count.bit_length() - 1
    gspec = pl.BlockSpec(grad_own.shape, lambda i: (0, 0, 0, 0))
    vspec = pl.BlockSpec((per, blocks, width, chan), lambda i: (i, 0, 0, 0))
    ospec = pl.BlockSpec((count // 2, unit // 2, tile), lambda i: (0, 0, i))
    shape = jax.ShapeDtypeStruct((count // 2, unit // 2, rows), F32)
    depth = 2 * blocks * chan
    return pl.pallas_call(
        functools.partial(first_kernel, bits),
        grid=(rows // tile,),
        in_specs=[pl.BlockSpec(memory_space=pltpu.SMEM), gspec, gspec, vspec, vspec],
        out_specs=[ospec] * 4,
        out_shape=[shape] * 4,
        scratch_shapes=[pltpu.VMEM((count * unit, depth), BF16)] * 2,
        compiler_params=params(),
        cost_estimate=cost(6 * rows * count * unit * depth, 4 * (rows * count * unit + 2 * rows * depth)),
        name="first",
    )(ids, grad_own, grad_other, v_own, v_other)


def body(seq_count, rep_count, inputs, gate_in, out_grad, w_first, w_second, w_out):
    total = w_second.shape[0]
    own = total // seq_count
    rows = inputs.shape[0] // own
    chan = inputs.shape[1]
    width = rows // seq_count
    unit, columns = w_first.shape
    bits = seq_count.bit_length() - 1
    s = lax.axis_index("seq").astype(jnp.int32)
    h = lax.axis_index("chan").astype(jnp.int32)
    side = lax.rem(lax.axis_index("rep").astype(jnp.int32), 2)
    ids = jnp.stack([s, h, side])
    group = 16 if total * 16 <= 256 else 8

    def swap_core(x):
        return lax.ppermute(x, "chan", [(0, 1), (1, 0)])

    def swap_rep(x):
        return lax.ppermute(x, "rep", [(i, i ^ 1) for i in range(rep_count)])

    def swap_seq(x, bit):
        return lax.ppermute(x, "seq", [(i, i ^ bit) for i in range(seq_count)])

    def exchange(x):
        return lax.all_to_all(x, "seq", split_axis=0, concat_axis=0, tiled=True)

    def after(x, *deps):
        return lax.optimization_barrier((x, *deps))[0]

    other_cot = swap_core(out_grad)
    half = lax.dynamic_slice_in_dim(w_first, side * (unit // 2), unit // 2, 0).reshape(1, unit // 2, columns)
    far_bits = range(2, seq_count, 2)
    z_all = jnp.concatenate([half] + [swap_seq(half, b) for b in far_bits], axis=0)
    z_rel = (0, *far_bits)

    own_rows = lax.dynamic_slice_in_dim(w_out, h * chan, chan, 0)
    w_cat = jnp.concatenate(
        [
            lax.dynamic_slice_in_dim(own_rows, h * chan, chan, 1),
            lax.dynamic_slice_in_dim(own_rows, (1 - h) * chan, chan, 1),
        ],
        axis=1,
    )
    grad, factor, grad_own, grad_send = gate_call(ids, out_grad, other_cot, gate_in, w_cat, own, unit)
    grad_other = swap_core(grad_send)
    mixers = spread_call(w_second, group)

    sliced = inputs.reshape(own, seq_count, width, chan).transpose(1, 0, 2, 3)
    block_cols = exchange(after(sliced, grad, z_all)).reshape(total, width, chan)

    n = len(z_rel)
    y_all = swap_seq(z_all, 1)
    x_all = swap_rep(z_all)
    yx_a = swap_seq(x_all[: n // 2], 1)
    yx_b = swap_rep(y_all[n // 2 :])
    pieces = [z_all, y_all, x_all, yx_a, yx_b]
    offsets = [
        [(r, 0, 0) for r in z_rel],
        [(r ^ 1, 0, 0) for r in z_rel],
        [(r, 0, 1) for r in z_rel],
        [(r ^ 1, 0, 1) for r in z_rel[: n // 2]],
        [(r ^ 1, 0, 1) for r in z_rel[n // 2 :]],
    ]

    block_cols = after(block_cols, y_all, x_all, grad_other)
    v_cols = mix_call(mixers[:2], block_cols, group)
    v = exchange(v_cols.reshape(seq_count, own, width, chan))

    far = [swap_core(p) for p in pieces[:3]] + [swap_core(after(p, v_cols)) for p in pieces[3:]]
    offsets += [[(r, 1, f) for r, _, f in o] for o in offsets]
    hi, lo = place_call(ids, pieces + far, tuple(map(tuple, offsets)), rows, columns)
    u = up_call(hi, lo, grad.reshape(own, rows, chan), seq_count)
    v = after(v, u)
    u_cols = exchange(u).reshape(total, width, chan)

    keep_a, send_a, keep_b, send_b = first_call(ids, grad_own, grad_other, v, swap_core(v))
    got_a, got_b = swap_seq(send_a, 1), swap_seq(send_b, 2)
    gate_grad = mixed_call(hi, lo, after(v, send_a), factor.reshape(own, rows, chan)).reshape(inputs.shape)
    keep_a, keep_b = keep_a + got_a, keep_b + got_b

    in_cols = mix_second_call(
        mixers[2:],
        after(u_cols, gate_grad, keep_a, keep_b),
        block_cols,
        group,
        own,
        1.0 / math.sqrt(rows * 2 * chan),
    )
    back = exchange(in_cols.reshape(seq_count, own, *in_cols.shape[1:]))
    input_grad = back[:, :, :width].transpose(1, 0, 2, 3).reshape(inputs.shape)
    second = jnp.sum(back[:, :, width:, :total], axis=0).reshape(total, total)
    second = second + swap_core(second)

    quarter = keep_a.shape[0] // 2
    got_a, got_b = swap_seq(keep_a[quarter:], 2), swap_seq(keep_b[quarter:], 1)
    keep = jnp.concatenate([keep_a[:quarter] + got_a, keep_b[:quarter] + got_b], axis=1)
    for b in range(2, bits):
        part = keep.shape[0] // 2
        keep = keep[:part] + swap_seq(keep[part:], 1 << b)
    first_grad = keep.reshape(unit, columns) * (1.0 / math.sqrt(total * 2 * chan))
    return input_grad, gate_grad, first_grad, second


def solution(mesh):
    return jax.shard_map(
        functools.partial(body, mesh.shape["seq"], mesh.shape["rep"]),
        mesh=mesh,
        in_specs=(
            P(("rep", "seq"), "chan"),
            P(("rep", "seq"), "chan"),
            P(("rep", "seq"), "chan"),
            P(("seq", "chan"), None),
            P(),
            P(),
        ),
        out_specs=(
            P(("rep", "seq"), "chan"),
            P(("rep", "seq"), "chan"),
            P(("rep", "seq", "chan"), None),
            P("rep", None),
        ),
        check_vma=False,
    )
```

```python
import functools
import math

import jax
import jax.numpy as jnp
from jax import lax
from jax.experimental import pallas as pl
from jax.experimental.pallas import tpu as pltpu
from jax.sharding import PartitionSpec as P

F32 = jnp.float32
BF16 = jnp.bfloat16
NN = (((1,), (0,)), ((), ()))
NT = (((1,), (1,)), ((), ()))
TN = (((0,), (0,)), ((), ()))
VMEM_LIMIT = 16 * 1024 * 1024


def split(x):
    hi = x.astype(BF16)
    return hi, (x - hi.astype(F32)).astype(BF16)


def dot3(a, b, dims):
    (ah, al), (bh, bl) = a, b

    def d(u, v):
        return lax.dot_general(u, v, dims, preferred_element_type=F32)

    return d(ah, bh) + (d(ah, bl) + d(al, bh))


def hbm(x):
    return pltpu.with_memory_space_constraint(x, pltpu.HBM)


def params():
    return pltpu.CompilerParams(vmem_limit_bytes=VMEM_LIMIT)


def cost(flops, size):
    return pl.CostEstimate(flops=flops, bytes_accessed=size, transcendentals=0)


def gate_kernel(ids_ref, own_ref, other_ref, gate_ref, w_ref, grad_ref, factor_ref, mine_ref, send_ref):
    cot = jnp.concatenate([own_ref[...], other_ref[...]], axis=1)
    hidden = dot3(split(cot), split(w_ref[...]), NT)
    g = gate_ref[...]
    s = jax.nn.sigmoid(g)
    hs = hidden * s
    grad = hs * g
    grad_ref[...] = grad
    _, count, unit, width = mine_ref.shape
    pairs = grad.reshape(count, 2, unit, width)
    low = ids_ref[1] == 0
    mine_ref[0] = jnp.where(low, pairs[:, 0], pairs[:, 1])
    send_ref[0] = jnp.where(low, pairs[:, 1], pairs[:, 0])
    factor_ref[...] = hs * (1.0 + g * (1.0 - s))


def gate_call(ids, own, other, gate, w, blocks, unit):
    rows, width = own.shape
    per = 2
    tile = rows // blocks // per
    count = tile // (2 * unit)
    row = pl.BlockSpec((tile, width), lambda i: (i, 0))
    part = pl.BlockSpec((1, count, unit, width), lambda i: (i // per, i % per, 0, 0))
    shape = pltpu.HBM(own.shape, F32)
    part_shape = pltpu.HBM((blocks, per * count, unit, width), F32)
    return pl.pallas_call(
        gate_kernel,
        grid=(blocks * per,),
        in_specs=[
            pl.BlockSpec(memory_space=pltpu.SMEM),
            row,
            row,
            row,
            pl.BlockSpec(w.shape, lambda i: (0, 0)),
        ],
        out_specs=[row, row, part, part],
        out_shape=[shape, shape, part_shape, part_shape],
        compiler_params=params(),
        cost_estimate=cost(6 * rows * width * 2 * width, 6 * 4 * rows * width),
        name="gate",
    )(ids, hbm(own), other, hbm(gate), w)


def grouped(ref, group):
    n, span, width = ref.shape
    return jnp.concatenate(
        [ref[:, g * group : (g + 1) * group, :].reshape(n * group, width) for g in range(span // group)], axis=1
    )


def scatter_groups(ref, group, val):
    n, span, width = ref.shape
    for g in range(span // group):
        ref[:, g * group : (g + 1) * group, :] = val[:, g * width : (g + 1) * width].reshape(n, group, width)


def spread(w, group):
    n = w.shape[0]
    size = n * group
    pick = (
        lax.div(lax.broadcasted_iota(jnp.int32, (size, n), 0), group)
        == lax.broadcasted_iota(jnp.int32, (size, n), 1)
    ).astype(F32)

    def d(a, b, dims):
        return lax.dot_general(a, b, dims, precision=lax.Precision.HIGHEST, preferred_element_type=F32)

    full = d(d(pick, w, NN), pick, NT)
    r = lax.broadcasted_iota(jnp.int32, (size, size), 0)
    c = lax.broadcasted_iota(jnp.int32, (size, size), 1)
    return jnp.where(lax.rem(r, group) == lax.rem(c, group), full, 0.0)


def spread_kernel(group, w_ref, kh, kl, th, tl):
    w = w_ref[...]
    kh[...], kl[...] = split(spread(w, group))
    th[...], tl[...] = split(spread(w.T, group))


def spread_call(w, group):
    size = w.shape[0] * group
    return pl.pallas_call(
        functools.partial(spread_kernel, group),
        out_shape=[pltpu.HBM((size, size), BF16)] * 4,
        compiler_params=params(),
        cost_estimate=cost(8 * size * size * w.shape[0], 8 * size * size),
        name="spread",
    )(w)


def spans(width, group):
    step = min(width, 2 * group)
    return [(a, step) for a in range(0, width, step)]


def mix_kernel(group, kh, kl, x_ref, o_ref):
    k = kh[...], kl[...]
    for a, step in spans(x_ref.shape[1], group):
        x = grouped(x_ref.at[:, a : a + step], group)
        scatter_groups(o_ref.at[:, a : a + step], group, dot3(k, split(x), NN))


def mix_second_kernel(group, scale, own, kh, kl, u_ref, b_ref, o_ref, acc):
    k = kh[...], kl[...]
    n, width, _ = u_ref.shape
    for a, step in spans(width, group):
        u = split(grouped(u_ref.at[:, a : a + step], group))
        b = split(grouped(b_ref.at[:, a : a + step], group))
        scatter_groups(o_ref.at[:, a : a + step], group, dot3(k, u, NN))
        term = dot3(u, b, NT)
        acc[...] = term if a == 0 else acc[...] + term
    size = n * group
    r = lax.broadcasted_iota(jnp.int32, (size, size), 0)
    c = lax.broadcasted_iota(jnp.int32, (size, size), 1)
    diag = jnp.where(lax.rem(r, group) == lax.rem(c, group), acc[...], 0.0)
    rows = jnp.sum(diag.reshape(n, group, size), axis=1)
    lanes = o_ref.shape[2]
    pick = (
        lax.div(lax.broadcasted_iota(jnp.int32, (size, lanes), 0), group)
        == lax.broadcasted_iota(jnp.int32, (size, lanes), 1)
    ).astype(F32)
    second = scale * jnp.dot(rows, pick, precision=lax.Precision.HIGHEST, preferred_element_type=F32)
    part = n // own
    for m in range(n):
        start = (m % own) * part
        o_ref[m, width:, :] = second[start : start + part, :]


def mix_call(k, x, group):
    n, width, chan = x.shape
    return pl.pallas_call(
        functools.partial(mix_kernel, group),
        out_shape=jax.ShapeDtypeStruct(x.shape, F32),
        compiler_params=params(),
        cost_estimate=cost(6 * group * n * n * width * chan, 8 * n * width * chan),
        name="mix",
    )(*k, x)


def mix_second_call(k, u, b, group, own, scale):
    n, width, chan = u.shape
    size = n * group
    return pl.pallas_call(
        functools.partial(mix_second_kernel, group, scale, own),
        out_shape=jax.ShapeDtypeStruct((n, width + n // own, chan), F32),
        scratch_shapes=[pltpu.VMEM((size, size), F32)],
        compiler_params=params(),
        cost_estimate=cost(12 * size * n * width * chan, 12 * n * width * chan),
        name="mix_second",
    )(*k, u, b)


def place_copies(offsets, ids_ref, pieces, whole, sem):
    half = pieces[0].shape[1]
    copies = []
    for piece, rels in zip(pieces, offsets):
        for u, (rel, side, flip) in enumerate(rels):
            place = 2 * lax.bitwise_xor(ids_ref[0], rel) + lax.bitwise_xor(ids_ref[1], side)
            place = 2 * place + lax.bitwise_xor(ids_ref[2], flip)
            start = pl.multiple_of(place * half, half)
            copies.append(pltpu.make_async_copy(piece.at[u], whole.at[pl.ds(start, half)], sem.at[len(copies)]))
    return copies


def up_kernel(offsets, ids_ref, g_ref, *refs):
    pieces = refs[: len(offsets)]
    o_ref, whole, g, o, sem, g_sem, o_sem = refs[len(offsets) :]
    loads = place_copies(offsets, ids_ref, pieces, whole, sem)
    g_load = pltpu.make_async_copy(g_ref, g, g_sem)
    g_load.start()
    for c in loads:
        c.start()
    g_load.wait()
    blocks, rows, chan = g.shape
    slices, _, width, _ = o.shape
    both = split(jnp.concatenate([g[m] for m in range(blocks)], axis=1))
    for c in loads:
        c.wait()
    tile = max(width, 256)
    per = tile // width
    stores = []
    for n in range(rows // tile):
        res = dot3(split(whole[:, n * tile : (n + 1) * tile]), both, TN)
        for t in range(per):
            for m in range(blocks):
                o[n * per + t, m] = res[t * width : (t + 1) * width, m * chan : (m + 1) * chan]
        part = pl.ds(n * per, per)
        stores.append(pltpu.make_async_copy(o.at[part], o_ref.at[part], o_sem.at[n]))
        stores[-1].start()
    for c in stores:
        c.wait()


def up_call(ids, pieces, offsets, grad, slices, columns):
    blocks, rows, chan = grad.shape
    shape = (slices, blocks, rows // slices, chan)
    space = pl.BlockSpec(memory_space=pltpu.HBM)
    return pl.pallas_call(
        functools.partial(up_kernel, offsets),
        in_specs=[pl.BlockSpec(memory_space=pltpu.SMEM)] + [space] * (1 + len(pieces)),
        out_specs=space,
        out_shape=pltpu.HBM(shape, F32),
        scratch_shapes=[
            pltpu.VMEM((rows, columns), F32),
            pltpu.VMEM(grad.shape, F32),
            pltpu.VMEM(shape, F32),
            pltpu.SemaphoreType.DMA((sum(map(len, offsets)),)),
            pltpu.SemaphoreType.DMA,
            pltpu.SemaphoreType.DMA((rows // 256,)),
        ],
        compiler_params=params(),
        cost_estimate=cost(6 * rows * rows * blocks * chan, 4 * rows * rows + 8 * rows * blocks * chan),
        name="up",
    )(ids, hbm(grad), *map(hbm, pieces))


def mixed_kernel(offsets, ids_ref, v_ref, f_ref, *refs):
    pieces = refs[: len(offsets)]
    o_ref, whole, v, f, o, sem, v_sem, o_sem = refs[len(offsets) :]
    loads = place_copies(offsets, ids_ref, pieces, whole, sem)
    v_loads = [
        pltpu.make_async_copy(v_ref, v, v_sem.at[0]),
        pltpu.make_async_copy(f_ref, f, v_sem.at[1]),
    ]
    for c in v_loads + loads:
        c.start()
    for c in v_loads:
        c.wait()
    slices, blocks, _, chan = v.shape
    both = split(
        jnp.concatenate(
            [jnp.concatenate([v[t, m] for m in range(blocks)], axis=1) for t in range(slices)], axis=0
        )
    )
    for c in loads:
        c.wait()
    rows = whole.shape[0]
    tile = 256
    stores = []
    for n in range(rows // tile):
        part = pl.ds(n * tile, tile)
        res = dot3(split(whole[part, :]), both, NN)
        for m in range(blocks):
            o[m, part, :] = res[:, m * chan : (m + 1) * chan] * f[m, part, :]
        stores.append(pltpu.make_async_copy(o.at[:, part], o_ref.at[:, part], o_sem.at[n]))
        stores[-1].start()
    for c in stores:
        c.wait()


def mixed_call(ids, pieces, offsets, v, factor, columns):
    blocks, rows, chan = factor.shape
    space = pl.BlockSpec(memory_space=pltpu.HBM)
    return pl.pallas_call(
        functools.partial(mixed_kernel, offsets),
        in_specs=[pl.BlockSpec(memory_space=pltpu.SMEM), pl.BlockSpec(memory_space=pl.ANY)]
        + [space] * (1 + len(pieces)),
        out_specs=space,
        out_shape=pltpu.HBM(factor.shape, F32),
        scratch_shapes=[
            pltpu.VMEM((rows, columns), F32),
            pltpu.VMEM(v.shape, F32),
            pltpu.VMEM(factor.shape, F32),
            pltpu.VMEM(factor.shape, F32),
            pltpu.SemaphoreType.DMA((sum(map(len, offsets)),)),
            pltpu.SemaphoreType.DMA((2,)),
            pltpu.SemaphoreType.DMA((rows // 256,)),
        ],
        compiler_params=params(),
        cost_estimate=cost(6 * rows * rows * blocks * chan, 4 * rows * rows + 12 * rows * blocks * chan),
        name="mixed",
    )(ids, v, hbm(factor), *map(hbm, pieces))


def flip_bits(q, bits):
    r = 0
    for b in range(bits):
        r |= ((q >> b) & 1) << (bits - 1 - b)
    return r


def first_kernel(bits, ids_ref, ga_ref, gb_ref, va_ref, vb_ref, ka_ref, sa_ref, kb_ref, sb_ref, lh, ll):
    count, unit = ga_ref.shape[1], ga_ref.shape[2]
    blocks = ga_ref.shape[0]

    @pl.when(pl.program_id(0) == 0)
    def _():
        for q in range(count):
            src = lax.bitwise_xor(ids_ref[0], flip_bits(q, bits))
            row = jnp.concatenate([r[m, src] for m in range(blocks) for r in (ga_ref, gb_ref)], axis=1)
            lh[q * unit : (q + 1) * unit, :], ll[q * unit : (q + 1) * unit, :] = split(row)

    v = jnp.concatenate(
        [
            jnp.concatenate([r[t, m] for m in range(blocks) for r in (va_ref, vb_ref)], axis=1)
            for t in range(va_ref.shape[0])
        ],
        axis=0,
    )
    res = dot3((lh[...], ll[...]), split(v), NT)
    quarter, half = count // 4, unit // 2
    for q in range(count):
        r0, r1, rest = q // (2 * quarter), (q // quarter) % 2, q % quarter
        (sa_ref if r0 else ka_ref)[r1 * quarter + rest] = res[q * unit : q * unit + half, :]
        (sb_ref if r1 else kb_ref)[r0 * quarter + rest] = res[q * unit + half : (q + 1) * unit, :]


def first_call(ids, grad_own, grad_other, v_own, v_other):
    blocks, count, unit, chan = grad_own.shape
    slices, _, width, _ = v_own.shape
    rows = slices * width
    tile = 256
    per = tile // width
    bits = count.bit_length() - 1
    gspec = pl.BlockSpec(grad_own.shape, lambda i: (0, 0, 0, 0))
    vspec = pl.BlockSpec((per, blocks, width, chan), lambda i: (i, 0, 0, 0))
    ospec = pl.BlockSpec((count // 2, unit // 2, tile), lambda i: (0, 0, i))
    shape = jax.ShapeDtypeStruct((count // 2, unit // 2, rows), F32)
    depth = 2 * blocks * chan
    return pl.pallas_call(
        functools.partial(first_kernel, bits),
        grid=(rows // tile,),
        in_specs=[pl.BlockSpec(memory_space=pltpu.SMEM), gspec, gspec, vspec, vspec],
        out_specs=[ospec] * 4,
        out_shape=[shape] * 4,
        scratch_shapes=[pltpu.VMEM((count * unit, depth), BF16)] * 2,
        compiler_params=params(),
        cost_estimate=cost(6 * rows * count * unit * depth, 4 * (rows * count * unit + 2 * rows * depth)),
        name="first",
    )(ids, hbm(grad_own), grad_other, v_own, v_other)


def body(seq_count, rep_count, inputs, gate_in, out_grad, w_first, w_second, w_out):
    total = w_second.shape[0]
    own = total // seq_count
    rows = inputs.shape[0] // own
    chan = inputs.shape[1]
    width = rows // seq_count
    unit, columns = w_first.shape
    bits = seq_count.bit_length() - 1
    s = lax.axis_index("seq").astype(jnp.int32)
    h = lax.axis_index("chan").astype(jnp.int32)
    side = lax.rem(lax.axis_index("rep").astype(jnp.int32), 2)
    ids = jnp.stack([s, h, side])
    group = 16 if total * 16 <= 256 else 8

    def swap_core(x):
        return lax.ppermute(x, "chan", [(0, 1), (1, 0)])

    def swap_rep(x):
        return lax.ppermute(x, "rep", [(i, i ^ 1) for i in range(rep_count)])

    def swap_seq(x, bit):
        return lax.ppermute(x, "seq", [(i, i ^ bit) for i in range(seq_count)])

    def exchange(x):
        return lax.all_to_all(x, "seq", split_axis=0, concat_axis=0, tiled=True)

    def after(x, *deps):
        return lax.optimization_barrier((x, *deps))[0]

    other_cot = swap_core(out_grad)
    half = lax.dynamic_slice_in_dim(w_first, side * (unit // 2), unit // 2, 0).reshape(1, unit // 2, columns)
    far_bits = range(2, seq_count, 2)
    z_far = [swap_seq(half, b) for b in far_bits]
    z_rel = (0, *far_bits)

    own_rows = lax.dynamic_slice_in_dim(w_out, h * chan, chan, 0)
    w_cat = jnp.concatenate(
        [
            lax.dynamic_slice_in_dim(own_rows, h * chan, chan, 1),
            lax.dynamic_slice_in_dim(own_rows, (1 - h) * chan, chan, 1),
        ],
        axis=1,
    )
    grad, factor, grad_own, grad_send = gate_call(ids, out_grad, other_cot, gate_in, w_cat, own, unit)
    grad_other = swap_core(grad_send)
    mixers = spread_call(w_second, group)
    z_all = jnp.concatenate([after(half, grad, mixers[0])] + z_far, axis=0)

    sliced = inputs.reshape(own, seq_count, width, chan).transpose(1, 0, 2, 3)
    block_cols = exchange(after(sliced, z_all)).reshape(total, width, chan)

    y_all = swap_seq(z_all, 1)
    x_all = swap_rep(z_all)
    yx_all = swap_rep(y_all)
    pieces = [z_all, y_all, x_all, yx_all]
    offsets = [
        [(r, 0, 0) for r in z_rel],
        [(r ^ 1, 0, 0) for r in z_rel],
        [(r, 0, 1) for r in z_rel],
        [(r ^ 1, 0, 1) for r in z_rel],
    ]

    block_cols = after(block_cols, y_all, x_all, grad_other)
    v_cols = mix_call(mixers[:2], block_cols, group)
    v = exchange(v_cols.reshape(seq_count, own, width, chan))

    far = [swap_core(p) for p in pieces[:3]] + [swap_core(after(p, v_cols)) for p in pieces[3:]]
    offsets += [[(r, 1, f) for r, _, f in o] for o in offsets]
    pieces += far
    offsets = tuple(map(tuple, offsets))
    u = up_call(ids, pieces, offsets, grad.reshape(own, rows, chan), seq_count, columns)
    v = after(v, u)
    u_cols = exchange(u).reshape(total, width, chan)

    keep_a, send_a, keep_b, send_b = first_call(ids, grad_own, grad_other, v, swap_core(v))
    got_a, got_b = swap_seq(send_a, 1), swap_seq(send_b, 2)
    gate_grad = mixed_call(
        ids, pieces, offsets, after(v, send_a), factor.reshape(own, rows, chan), columns
    ).reshape(inputs.shape)
    keep_a, keep_b = keep_a + got_a, keep_b + got_b

    in_cols = mix_second_call(
        mixers[2:],
        after(u_cols, gate_grad, keep_a, keep_b),
        block_cols,
        group,
        own,
        1.0 / math.sqrt(rows * 2 * chan),
    )
    back = exchange(in_cols.reshape(seq_count, own, *in_cols.shape[1:]))
    input_grad = back[:, :, :width].transpose(1, 0, 2, 3).reshape(inputs.shape)
    second = jnp.sum(back[:, :, width:, :total], axis=0).reshape(total, total)
    second = second + swap_core(second)

    quarter = keep_a.shape[0] // 2
    got_a, got_b = swap_seq(keep_a[quarter:], 2), swap_seq(keep_b[quarter:], 1)
    keep = jnp.concatenate([keep_a[:quarter] + got_a, keep_b[:quarter] + got_b], axis=1)
    for b in range(2, bits):
        part = keep.shape[0] // 2
        keep = keep[:part] + swap_seq(keep[part:], 1 << b)
    first_grad = keep.reshape(unit, columns) * (1.0 / math.sqrt(total * 2 * chan))
    return input_grad, gate_grad, first_grad, second


def solution(mesh):
    return jax.shard_map(
        functools.partial(body, mesh.shape["seq"], mesh.shape["rep"]),
        mesh=mesh,
        in_specs=(
            P(("rep", "seq"), "chan"),
            P(("rep", "seq"), "chan"),
            P(("rep", "seq"), "chan"),
            P(("seq", "chan"), None),
            P(),
            P(),
        ),
        out_specs=(
            P(("rep", "seq"), "chan"),
            P(("rep", "seq"), "chan"),
            P(("rep", "seq", "chan"), None),
            P("rep", None),
        ),
        check_vma=False,
    )
```

```python
import functools
import math

import jax
import jax.numpy as jnp
from jax import lax
from jax.experimental import pallas as pl
from jax.experimental.pallas import tpu as pltpu
from jax.sharding import PartitionSpec as P

F32 = jnp.float32
BF16 = jnp.bfloat16
NN = (((1,), (0,)), ((), ()))
NT = (((1,), (1,)), ((), ()))
TN = (((0,), (0,)), ((), ()))
VMEM_LIMIT = 16 * 1024 * 1024


def split(x):
    hi = x.astype(BF16)
    return hi, (x - hi.astype(F32)).astype(BF16)


def dot3(a, b, dims):
    (ah, al), (bh, bl) = a, b

    def d(u, v):
        return lax.dot_general(u, v, dims, preferred_element_type=F32)

    return d(ah, bh) + (d(ah, bl) + d(al, bh))


def hbm(x):
    return pltpu.with_memory_space_constraint(x, pltpu.HBM)


def params():
    return pltpu.CompilerParams(vmem_limit_bytes=VMEM_LIMIT)


def cost(flops, size):
    return pl.CostEstimate(flops=flops, bytes_accessed=size, transcendentals=0)


def gate_kernel(ids_ref, own_ref, other_ref, gate_ref, w_ref, grad_ref, factor_ref, mine_ref, send_ref):
    cot = jnp.concatenate([own_ref[...], other_ref[...]], axis=1)
    hidden = dot3(split(cot), split(w_ref[...]), NT)
    g = gate_ref[...]
    s = jax.nn.sigmoid(g)
    hs = hidden * s
    grad = hs * g
    grad_ref[...] = grad
    _, count, unit, width = mine_ref.shape
    pairs = grad.reshape(count, 2, unit, width)
    low = ids_ref[1] == 0
    mine_ref[0] = jnp.where(low, pairs[:, 0], pairs[:, 1])
    send_ref[0] = jnp.where(low, pairs[:, 1], pairs[:, 0])
    factor_ref[...] = hs * (1.0 + g * (1.0 - s))


def gate_call(ids, own, other, gate, w, blocks, unit):
    rows, width = own.shape
    per = 2
    tile = rows // blocks // per
    count = tile // (2 * unit)
    row = pl.BlockSpec((tile, width), lambda i: (i, 0))
    part = pl.BlockSpec((1, count, unit, width), lambda i: (i // per, i % per, 0, 0))
    shape = pltpu.HBM(own.shape, F32)
    part_shape = pltpu.HBM((blocks, per * count, unit, width), F32)
    return pl.pallas_call(
        gate_kernel,
        grid=(blocks * per,),
        in_specs=[
            pl.BlockSpec(memory_space=pltpu.SMEM),
            row,
            row,
            row,
            pl.BlockSpec(w.shape, lambda i: (0, 0)),
        ],
        out_specs=[row, row, part, part],
        out_shape=[shape, shape, part_shape, part_shape],
        compiler_params=params(),
        cost_estimate=cost(6 * rows * width * 2 * width, 6 * 4 * rows * width),
        name="gate",
    )(ids, hbm(own), other, hbm(gate), w)


def grouped(ref, group):
    n, span, width = ref.shape
    return jnp.concatenate(
        [ref[:, g * group : (g + 1) * group, :].reshape(n * group, width) for g in range(span // group)], axis=1
    )


def scatter_groups(ref, group, val):
    n, span, width = ref.shape
    for g in range(span // group):
        ref[:, g * group : (g + 1) * group, :] = val[:, g * width : (g + 1) * width].reshape(n, group, width)


def spread(w, group):
    n = w.shape[0]
    size = n * group
    pick = (
        lax.div(lax.broadcasted_iota(jnp.int32, (size, n), 0), group)
        == lax.broadcasted_iota(jnp.int32, (size, n), 1)
    ).astype(F32)

    def d(a, b, dims):
        return lax.dot_general(a, b, dims, precision=lax.Precision.HIGHEST, preferred_element_type=F32)

    full = d(d(pick, w, NN), pick, NT)
    r = lax.broadcasted_iota(jnp.int32, (size, size), 0)
    c = lax.broadcasted_iota(jnp.int32, (size, size), 1)
    return jnp.where(lax.rem(r, group) == lax.rem(c, group), full, 0.0)


def spread_kernel(group, w_ref, kh, kl, th, tl):
    w = w_ref[...]
    kh[...], kl[...] = split(spread(w, group))
    th[...], tl[...] = split(spread(w.T, group))


def spread_call(w, group):
    size = w.shape[0] * group
    return pl.pallas_call(
        functools.partial(spread_kernel, group),
        out_shape=[pltpu.HBM((size, size), BF16)] * 4,
        compiler_params=params(),
        cost_estimate=cost(8 * size * size * w.shape[0], 8 * size * size),
        name="spread",
    )(w)


def spans(width, group):
    step = min(width, 2 * group)
    return [(a, step) for a in range(0, width, step)]


def mix_kernel(group, kh, kl, x_ref, o_ref):
    k = kh[...], kl[...]
    for a, step in spans(x_ref.shape[1], group):
        x = grouped(x_ref.at[:, a : a + step], group)
        scatter_groups(o_ref.at[:, a : a + step], group, dot3(k, split(x), NN))


def scatter_rows(ids_ref, ref, pieces):
    own = pieces[0].shape[0]
    for d, piece in enumerate(pieces):
        piece[...] = ref[pl.ds(own * lax.bitwise_xor(ids_ref[0], d), own)]


def mix_second_kernel(group, scale, count, ids_ref, kh, kl, u_ref, b_ref, *refs):
    outs, (o_ref, acc) = refs[:count], refs[count:]
    k = kh[...], kl[...]
    n, width, _ = u_ref.shape
    for a, step in spans(width, group):
        u = split(grouped(u_ref.at[:, a : a + step], group))
        b = split(grouped(b_ref.at[:, a : a + step], group))
        scatter_groups(o_ref.at[:, a : a + step], group, dot3(k, u, NN))
        term = dot3(u, b, NT)
        acc[...] = term if a == 0 else acc[...] + term
    size = n * group
    r = lax.broadcasted_iota(jnp.int32, (size, size), 0)
    c = lax.broadcasted_iota(jnp.int32, (size, size), 1)
    diag = jnp.where(lax.rem(r, group) == lax.rem(c, group), acc[...], 0.0)
    rows = jnp.sum(diag.reshape(n, group, size), axis=1)
    lanes = o_ref.shape[2]
    pick = (
        lax.div(lax.broadcasted_iota(jnp.int32, (size, lanes), 0), group)
        == lax.broadcasted_iota(jnp.int32, (size, lanes), 1)
    ).astype(F32)
    second = scale * jnp.dot(rows, pick, precision=lax.Precision.HIGHEST, preferred_element_type=F32)
    own = n // count
    part = n // own
    for m in range(n):
        start = (m % own) * part
        o_ref[m, width:, :] = second[start : start + part, :]
    scatter_rows(ids_ref, o_ref, outs)


def mix_call(k, x, group):
    n, width, chan = x.shape
    return pl.pallas_call(
        functools.partial(mix_kernel, group),
        out_shape=jax.ShapeDtypeStruct(x.shape, F32),
        compiler_params=params(),
        cost_estimate=cost(6 * group * n * n * width * chan, 8 * n * width * chan),
        name="mix",
    )(*k, x)


SMEM_SPEC = pl.BlockSpec(memory_space=pltpu.SMEM)
VMEM_SPEC = pl.BlockSpec(memory_space=pltpu.VMEM)


def mix_second_call(ids, k, u, b, group, count, scale):
    n, width, chan = u.shape
    own = n // count
    size = n * group
    tall = width + n // own
    return pl.pallas_call(
        functools.partial(mix_second_kernel, group, scale, count),
        in_specs=[SMEM_SPEC] + [VMEM_SPEC] * 4,
        out_specs=[VMEM_SPEC] * count,
        out_shape=[jax.ShapeDtypeStruct((own, tall, chan), F32)] * count,
        scratch_shapes=[pltpu.VMEM((n, tall, chan), F32), pltpu.VMEM((size, size), F32)],
        compiler_params=params(),
        cost_estimate=cost(12 * size * n * width * chan, 12 * n * width * chan),
        name="mix_second",
    )(ids, *k, u, b)


def finish_kernel(width, ids_ref, *refs):
    pieces, (o_ref, s_ref, sem) = refs[:-3], refs[-3:]
    copies = []
    for d, piece in enumerate(pieces):
        start = pl.multiple_of(lax.bitwise_xor(ids_ref[0], d) * width, width)
        copies.append(
            pltpu.make_async_copy(piece.at[:, :width], o_ref.at[:, pl.ds(start, width)], sem.at[d])
        )
    for c in copies:
        c.start()
    total = pieces[0][:, width:, :]
    for piece in pieces[1:]:
        total = total + piece[:, width:, :]
    s_ref[...] = total
    for c in copies:
        c.wait()


def finish_call(ids, pieces, width):
    own, tall, chan = pieces[0].shape
    count = len(pieces)
    return pl.pallas_call(
        functools.partial(finish_kernel, width),
        in_specs=[SMEM_SPEC] + [VMEM_SPEC] * count,
        out_specs=[pl.BlockSpec(memory_space=pltpu.HBM), VMEM_SPEC],
        out_shape=[
            pltpu.HBM((own, count * width, chan), F32),
            jax.ShapeDtypeStruct((own, tall - width, chan), F32),
        ],
        scratch_shapes=[pltpu.SemaphoreType.DMA((count,))],
        compiler_params=params(),
        cost_estimate=cost(0, 8 * own * tall * count * chan),
        name="finish",
    )(ids, *pieces)


def place_copies(offsets, ids_ref, pieces, whole, sem):
    half = pieces[0].shape[1]
    copies = []
    for piece, rels in zip(pieces, offsets):
        for u, (rel, side, flip) in enumerate(rels):
            place = 2 * lax.bitwise_xor(ids_ref[0], rel) + lax.bitwise_xor(ids_ref[1], side)
            place = 2 * place + lax.bitwise_xor(ids_ref[2], flip)
            start = pl.multiple_of(place * half, half)
            copies.append(pltpu.make_async_copy(piece.at[u], whole.at[pl.ds(start, half)], sem.at[len(copies)]))
    return copies


def up_kernel(offsets, ids_ref, g_ref, *refs):
    pieces = refs[: len(offsets)]
    o_ref, whole, g, o, sem, g_sem, o_sem = refs[len(offsets) :]
    loads = place_copies(offsets, ids_ref, pieces, whole, sem)
    g_load = pltpu.make_async_copy(g_ref, g, g_sem)
    g_load.start()
    for c in loads:
        c.start()
    g_load.wait()
    blocks, rows, chan = g.shape
    slices, _, width, _ = o.shape
    both = split(jnp.concatenate([g[m] for m in range(blocks)], axis=1))
    for c in loads:
        c.wait()
    tile = max(width, 256)
    per = tile // width
    stores = []
    for n in range(rows // tile):
        res = dot3(split(whole[:, n * tile : (n + 1) * tile]), both, TN)
        for t in range(per):
            for m in range(blocks):
                o[n * per + t, m] = res[t * width : (t + 1) * width, m * chan : (m + 1) * chan]
        part = pl.ds(n * per, per)
        stores.append(pltpu.make_async_copy(o.at[part], o_ref.at[part], o_sem.at[n]))
        stores[-1].start()
    for c in stores:
        c.wait()


def up_call(ids, pieces, offsets, grad, slices, columns):
    blocks, rows, chan = grad.shape
    shape = (slices, blocks, rows // slices, chan)
    space = pl.BlockSpec(memory_space=pltpu.HBM)
    return pl.pallas_call(
        functools.partial(up_kernel, offsets),
        in_specs=[pl.BlockSpec(memory_space=pltpu.SMEM)] + [space] * (1 + len(pieces)),
        out_specs=space,
        out_shape=pltpu.HBM(shape, F32),
        scratch_shapes=[
            pltpu.VMEM((rows, columns), F32),
            pltpu.VMEM(grad.shape, F32),
            pltpu.VMEM(shape, F32),
            pltpu.SemaphoreType.DMA((sum(map(len, offsets)),)),
            pltpu.SemaphoreType.DMA,
            pltpu.SemaphoreType.DMA((rows // 256,)),
        ],
        compiler_params=params(),
        cost_estimate=cost(6 * rows * rows * blocks * chan, 4 * rows * rows + 8 * rows * blocks * chan),
        name="up",
    )(ids, hbm(grad), *map(hbm, pieces))


def mixed_kernel(offsets, ids_ref, v_ref, f_ref, *refs):
    pieces = refs[: len(offsets)]
    o_ref, whole, v, f, o, sem, v_sem, o_sem = refs[len(offsets) :]
    loads = place_copies(offsets, ids_ref, pieces, whole, sem)
    v_loads = [
        pltpu.make_async_copy(v_ref, v, v_sem.at[0]),
        pltpu.make_async_copy(f_ref, f, v_sem.at[1]),
    ]
    for c in v_loads + loads:
        c.start()
    for c in v_loads:
        c.wait()
    slices, blocks, _, chan = v.shape
    both = split(
        jnp.concatenate(
            [jnp.concatenate([v[t, m] for m in range(blocks)], axis=1) for t in range(slices)], axis=0
        )
    )
    for c in loads:
        c.wait()
    rows = whole.shape[0]
    tile = 256
    stores = []
    for n in range(rows // tile):
        part = pl.ds(n * tile, tile)
        res = dot3(split(whole[part, :]), both, NN)
        for m in range(blocks):
            o[m, part, :] = res[:, m * chan : (m + 1) * chan] * f[m, part, :]
        stores.append(pltpu.make_async_copy(o.at[:, part], o_ref.at[:, part], o_sem.at[n]))
        stores[-1].start()
    for c in stores:
        c.wait()


def mixed_call(ids, pieces, offsets, v, factor, columns):
    blocks, rows, chan = factor.shape
    space = pl.BlockSpec(memory_space=pltpu.HBM)
    return pl.pallas_call(
        functools.partial(mixed_kernel, offsets),
        in_specs=[pl.BlockSpec(memory_space=pltpu.SMEM), pl.BlockSpec(memory_space=pl.ANY)]
        + [space] * (1 + len(pieces)),
        out_specs=space,
        out_shape=pltpu.HBM(factor.shape, F32),
        scratch_shapes=[
            pltpu.VMEM((rows, columns), F32),
            pltpu.VMEM(v.shape, F32),
            pltpu.VMEM(factor.shape, F32),
            pltpu.VMEM(factor.shape, F32),
            pltpu.SemaphoreType.DMA((sum(map(len, offsets)),)),
            pltpu.SemaphoreType.DMA((2,)),
            pltpu.SemaphoreType.DMA((rows // 256,)),
        ],
        compiler_params=params(),
        cost_estimate=cost(6 * rows * rows * blocks * chan, 4 * rows * rows + 12 * rows * blocks * chan),
        name="mixed",
    )(ids, v, hbm(factor), *map(hbm, pieces))


def flip_bits(q, bits):
    r = 0
    for b in range(bits):
        r |= ((q >> b) & 1) << (bits - 1 - b)
    return r


def first_kernel(
    bits, ids_ref, ga_hbm, gb_hbm, va_ref, vb_ref, ka_ref, sa_ref, kb_ref, sb_ref, ga_ref, gb_ref, lh, ll, sem
):
    blocks, count, unit, _ = ga_ref.shape
    loads = [
        pltpu.make_async_copy(ga_hbm, ga_ref, sem.at[0]),
        pltpu.make_async_copy(gb_hbm, gb_ref, sem.at[1]),
    ]
    for c in loads:
        c.start()
    for c in loads:
        c.wait()
    slices, _, width, _ = va_ref.shape
    for q in range(count):
        src = lax.bitwise_xor(ids_ref[0], flip_bits(q, bits))
        row = jnp.concatenate([r[m, src] for m in range(blocks) for r in (ga_ref, gb_ref)], axis=1)
        lh[q * unit : (q + 1) * unit, :], ll[q * unit : (q + 1) * unit, :] = split(row)
    left = lh[...], ll[...]
    quarter, half = count // 4, unit // 2
    tile = max(width, 256)
    per = tile // width
    for n in range(slices // per):
        v = jnp.concatenate(
            [
                jnp.concatenate([r[t, m] for m in range(blocks) for r in (va_ref, vb_ref)], axis=1)
                for t in range(n * per, (n + 1) * per)
            ],
            axis=0,
        )
        res = dot3(left, split(v), NT)
        part = slice(n * tile, (n + 1) * tile)
        for q in range(count):
            r0, r1, rest = q // (2 * quarter), (q // quarter) % 2, q % quarter
            (sa_ref if r0 else ka_ref)[r1 * quarter + rest, :, part] = res[q * unit : q * unit + half, :]
            (sb_ref if r1 else kb_ref)[r0 * quarter + rest, :, part] = res[q * unit + half : (q + 1) * unit, :]


def first_call(ids, grad_own, grad_other, v_own, v_other):
    blocks, count, unit, chan = grad_own.shape
    slices, _, width, _ = v_own.shape
    rows = slices * width
    bits = count.bit_length() - 1
    vmem = pl.BlockSpec(memory_space=pltpu.VMEM)
    shape = jax.ShapeDtypeStruct((count // 2, unit // 2, rows), F32)
    depth = 2 * blocks * chan
    return pl.pallas_call(
        functools.partial(first_kernel, bits),
        in_specs=[pl.BlockSpec(memory_space=pltpu.SMEM)]
        + [pl.BlockSpec(memory_space=pltpu.HBM)] * 2
        + [vmem] * 2,
        out_specs=[vmem] * 4,
        out_shape=[shape] * 4,
        scratch_shapes=[pltpu.VMEM(grad_own.shape, F32)] * 2
        + [pltpu.VMEM((count * unit, depth), BF16)] * 2
        + [pltpu.SemaphoreType.DMA((2,))],
        compiler_params=params(),
        cost_estimate=cost(6 * rows * count * unit * depth, 4 * (rows * count * unit + 2 * rows * depth)),
        name="first",
    )(ids, hbm(grad_own), hbm(grad_other), v_own, v_other)


def sums_kernel(ka_ref, ga_ref, kb_ref, gb_ref, oa_ref, sa_ref, ob_ref, sb_ref):
    half = oa_ref.shape[0]
    for k_ref, g_ref, o_ref, s_ref in ((ka_ref, ga_ref, oa_ref, sa_ref), (kb_ref, gb_ref, ob_ref, sb_ref)):
        s_ref[...] = k_ref[half:] + g_ref[half:]
        o_ref[...] = k_ref[:half] + g_ref[:half]


def sums_call(keep_a, got_a, keep_b, got_b):
    half, unit, columns = keep_a.shape[0] // 2, *keep_a.shape[1:]
    shape = jax.ShapeDtypeStruct((half, unit, columns), F32)
    return pl.pallas_call(
        sums_kernel,
        in_specs=[VMEM_SPEC] * 4,
        out_specs=[VMEM_SPEC] * 4,
        out_shape=[shape] * 4,
        compiler_params=params(),
        cost_estimate=cost(4 * half * unit * columns, 48 * half * unit * columns),
        name="sums",
    )(keep_a, got_a, keep_b, got_b)


def body(seq_count, rep_count, inputs, gate_in, out_grad, w_first, w_second, w_out):
    total = w_second.shape[0]
    own = total // seq_count
    rows = inputs.shape[0] // own
    chan = inputs.shape[1]
    width = rows // seq_count
    unit, columns = w_first.shape
    bits = seq_count.bit_length() - 1
    s = lax.axis_index("seq").astype(jnp.int32)
    h = lax.axis_index("chan").astype(jnp.int32)
    side = lax.rem(lax.axis_index("rep").astype(jnp.int32), 2)
    ids = jnp.stack([s, h, side])
    group = 16 if total * 16 <= 256 else 8

    def swap_core(x):
        return lax.ppermute(x, "chan", [(0, 1), (1, 0)])

    def swap_rep(x):
        return lax.ppermute(x, "rep", [(i, i ^ 1) for i in range(rep_count)])

    def swap_seq(x, bit):
        return lax.ppermute(x, "seq", [(i, i ^ bit) for i in range(seq_count)])

    def exchange(x):
        return lax.all_to_all(x, "seq", split_axis=0, concat_axis=0, tiled=True)

    def after(x, *deps):
        return lax.optimization_barrier((x, *deps))[0]

    def all_after(xs, *deps):
        return lax.optimization_barrier((*xs, *deps))[: len(xs)]

    other_cot = swap_core(out_grad)
    half = lax.dynamic_slice_in_dim(w_first, side * (unit // 2), unit // 2, 0).reshape(1, unit // 2, columns)
    far_bits = range(2, seq_count, 2)
    z_far = [swap_seq(half, b) for b in far_bits]
    z_rel = (0, *far_bits)

    own_rows = lax.dynamic_slice_in_dim(w_out, h * chan, chan, 0)
    w_cat = jnp.concatenate(
        [
            lax.dynamic_slice_in_dim(own_rows, h * chan, chan, 1),
            lax.dynamic_slice_in_dim(own_rows, (1 - h) * chan, chan, 1),
        ],
        axis=1,
    )
    grad, factor, grad_own, grad_send = gate_call(ids, out_grad, other_cot, gate_in, w_cat, own, unit)
    grad_other = swap_core(grad_send)
    mixers = spread_call(w_second, group)
    z_all = jnp.concatenate([after(half, grad, mixers[0])] + z_far, axis=0)

    sliced = inputs.reshape(own, seq_count, width, chan).transpose(1, 0, 2, 3)
    block_cols = exchange(after(sliced, z_all)).reshape(total, width, chan)

    y_all = swap_seq(z_all, 1)
    x_all = swap_rep(z_all)
    yx_all = swap_rep(y_all)
    pieces = [z_all, y_all, x_all, yx_all]
    offsets = [
        [(r, 0, 0) for r in z_rel],
        [(r ^ 1, 0, 0) for r in z_rel],
        [(r, 0, 1) for r in z_rel],
        [(r ^ 1, 0, 1) for r in z_rel],
    ]

    block_cols = after(block_cols, y_all, x_all, grad_other)
    v_cols = mix_call(mixers[:2], block_cols, group)
    v = exchange(v_cols.reshape(seq_count, own, width, chan))

    far = [swap_core(p) for p in pieces[:3]] + [swap_core(after(p, v_cols)) for p in pieces[3:]]
    offsets += [[(r, 1, f) for r, _, f in o] for o in offsets]
    pieces += far
    offsets = tuple(map(tuple, offsets))
    u = up_call(ids, pieces, offsets, grad.reshape(own, rows, chan), seq_count, columns)
    v = after(v, u)
    u_cols = exchange(u).reshape(total, width, chan)

    keep_a, send_a, keep_b, send_b = first_call(ids, grad_own, grad_other, v, swap_core(v))
    got_a, got_b = swap_seq(send_a, 1), swap_seq(send_b, 2)
    gate_grad = mixed_call(
        ids, pieces, offsets, after(v, send_a), factor.reshape(own, rows, chan), columns
    ).reshape(inputs.shape)

    in_pieces = mix_second_call(
        ids,
        mixers[2:],
        after(u_cols, gate_grad),
        block_cols,
        group,
        seq_count,
        1.0 / math.sqrt(rows * 2 * chan),
    )
    got_a, got_b = all_after([got_a, got_b], in_pieces[0])
    keep_a, send_a, keep_b, send_b = sums_call(keep_a, got_a, keep_b, got_b)
    got_a, got_b = swap_seq(send_a, 2), swap_seq(send_b, 1)

    back = {0: in_pieces[0]}
    for d in reversed(range(1, seq_count)):
        piece = in_pieces[d] if 2 * d >= seq_count else after(in_pieces[d], got_a, got_b)
        back[d] = swap_seq(piece, d)

    keep = jnp.concatenate([keep_a + got_a, keep_b + got_b], axis=1)
    for b in range(2, bits):
        part = keep.shape[0] // 2
        keep = keep[:part] + swap_seq(keep[part:], 1 << b)
    first_grad = keep.reshape(unit, columns) * (1.0 / math.sqrt(total * 2 * chan))

    input_grad, second = finish_call(ids, [back[d] for d in range(seq_count)], width)
    input_grad = input_grad.reshape(inputs.shape)
    second = second[:, :, :total].reshape(total, total)
    second = second + swap_core(second)
    return input_grad, gate_grad, first_grad, second


def solution(mesh):
    return jax.shard_map(
        functools.partial(body, mesh.shape["seq"], mesh.shape["rep"]),
        mesh=mesh,
        in_specs=(
            P(("rep", "seq"), "chan"),
            P(("rep", "seq"), "chan"),
            P(("rep", "seq"), "chan"),
            P(("seq", "chan"), None),
            P(),
            P(),
        ),
        out_specs=(
            P(("rep", "seq"), "chan"),
            P(("rep", "seq"), "chan"),
            P(("rep", "seq", "chan"), None),
            P("rep", None),
        ),
        check_vma=False,
    )
```

```python
import functools
import math

import jax
import jax.numpy as jnp
from jax import lax
from jax.experimental import pallas as pl
from jax.experimental.pallas import tpu as pltpu
from jax.sharding import PartitionSpec as P

F32 = jnp.float32
BF16 = jnp.bfloat16
NN = (((1,), (0,)), ((), ()))
NT = (((1,), (1,)), ((), ()))
TN = (((0,), (0,)), ((), ()))
VMEM_LIMIT = 16 * 1024 * 1024


def split(x):
    hi = x.astype(BF16)
    return hi, (x - hi.astype(F32)).astype(BF16)


def dot3(a, b, dims):
    (ah, al), (bh, bl) = a, b

    def d(u, v):
        return lax.dot_general(u, v, dims, preferred_element_type=F32)

    return d(ah, bh) + (d(ah, bl) + d(al, bh))


def hbm(x):
    return pltpu.with_memory_space_constraint(x, pltpu.HBM)


def params():
    return pltpu.CompilerParams(vmem_limit_bytes=VMEM_LIMIT)


def cost(flops, size):
    return pl.CostEstimate(flops=flops, bytes_accessed=size, transcendentals=0)


def gate_kernel(ids_ref, own_ref, other_ref, gate_ref, w_ref, grad_ref, factor_ref, mine_ref, send_ref):
    cot = jnp.concatenate([own_ref[...], other_ref[...]], axis=1)
    hidden = dot3(split(cot), split(w_ref[...]), NT)
    g = gate_ref[...]
    s = jax.nn.sigmoid(g)
    hs = hidden * s
    grad = hs * g
    grad_ref[...] = grad
    _, count, unit, width = mine_ref.shape
    pairs = grad.reshape(count, 2, unit, width)
    low = ids_ref[1] == 0
    mine_ref[0] = jnp.where(low, pairs[:, 0], pairs[:, 1])
    send_ref[0] = jnp.where(low, pairs[:, 1], pairs[:, 0])
    factor_ref[...] = hs * (1.0 + g * (1.0 - s))


def gate_call(ids, own, other, gate, w, blocks, unit):
    rows, width = own.shape
    per = 2
    tile = rows // blocks // per
    count = tile // (2 * unit)
    row = pl.BlockSpec((tile, width), lambda i: (i, 0))
    part = pl.BlockSpec((1, count, unit, width), lambda i: (i // per, i % per, 0, 0))
    shape = pltpu.HBM(own.shape, F32)
    part_shape = pltpu.HBM((blocks, per * count, unit, width), F32)
    return pl.pallas_call(
        gate_kernel,
        grid=(blocks * per,),
        in_specs=[
            pl.BlockSpec(memory_space=pltpu.SMEM),
            row,
            row,
            row,
            pl.BlockSpec(w.shape, lambda i: (0, 0)),
        ],
        out_specs=[row, row, part, part],
        out_shape=[shape, shape, part_shape, part_shape],
        compiler_params=params(),
        cost_estimate=cost(6 * rows * width * 2 * width, 6 * 4 * rows * width),
        name="gate",
    )(ids, hbm(own), other, hbm(gate), w)


def grouped(ref, group):
    n, span, width = ref.shape
    return jnp.concatenate(
        [ref[:, g * group : (g + 1) * group, :].reshape(n * group, width) for g in range(span // group)], axis=1
    )


def scatter_groups(ref, group, val):
    n, span, width = ref.shape
    for g in range(span // group):
        ref[:, g * group : (g + 1) * group, :] = val[:, g * width : (g + 1) * width].reshape(n, group, width)


def spread(w, group):
    n = w.shape[0]
    size = n * group
    pick = (
        lax.div(lax.broadcasted_iota(jnp.int32, (size, n), 0), group)
        == lax.broadcasted_iota(jnp.int32, (size, n), 1)
    ).astype(F32)

    def d(a, b, dims):
        return lax.dot_general(a, b, dims, precision=lax.Precision.HIGHEST, preferred_element_type=F32)

    full = d(d(pick, w, NN), pick, NT)
    r = lax.broadcasted_iota(jnp.int32, (size, size), 0)
    c = lax.broadcasted_iota(jnp.int32, (size, size), 1)
    return jnp.where(lax.rem(r, group) == lax.rem(c, group), full, 0.0)


def spread_kernel(group, w_ref, kh, kl, th, tl):
    w = w_ref[...]
    kh[...], kl[...] = split(spread(w, group))
    th[...], tl[...] = split(spread(w.T, group))


def spread_call(w, group):
    size = w.shape[0] * group
    return pl.pallas_call(
        functools.partial(spread_kernel, group),
        out_shape=[pltpu.HBM((size, size), BF16)] * 4,
        compiler_params=params(),
        cost_estimate=cost(8 * size * size * w.shape[0], 8 * size * size),
        name="spread",
    )(w)


def spans(width, group):
    step = min(width, 2 * group)
    return [(a, step) for a in range(0, width, step)]


def mix_kernel(group, kh, kl, x_ref, o_ref):
    k = kh[...], kl[...]
    for a, step in spans(x_ref.shape[1], group):
        x = grouped(x_ref.at[:, a : a + step], group)
        scatter_groups(o_ref.at[:, a : a + step], group, dot3(k, split(x), NN))


def scatter_rows(ids_ref, ref, pieces):
    own = pieces[0].shape[0]
    for d, piece in enumerate(pieces):
        piece[...] = ref[pl.ds(own * lax.bitwise_xor(ids_ref[0], d), own)]


def mix_second_kernel(group, scale, count, ids_ref, kh, kl, u_ref, b_ref, *refs):
    outs, (o_ref, acc) = refs[:count], refs[count:]
    k = kh[...], kl[...]
    n, width, _ = u_ref.shape
    for a, step in spans(width, group):
        u = split(grouped(u_ref.at[:, a : a + step], group))
        b = split(grouped(b_ref.at[:, a : a + step], group))
        scatter_groups(o_ref.at[:, a : a + step], group, dot3(k, u, NN))
        term = dot3(u, b, NT)
        acc[...] = term if a == 0 else acc[...] + term
    size = n * group
    r = lax.broadcasted_iota(jnp.int32, (size, size), 0)
    c = lax.broadcasted_iota(jnp.int32, (size, size), 1)
    diag = jnp.where(lax.rem(r, group) == lax.rem(c, group), acc[...], 0.0)
    rows = jnp.sum(diag.reshape(n, group, size), axis=1)
    lanes = o_ref.shape[2]
    pick = (
        lax.div(lax.broadcasted_iota(jnp.int32, (size, lanes), 0), group)
        == lax.broadcasted_iota(jnp.int32, (size, lanes), 1)
    ).astype(F32)
    second = scale * jnp.dot(rows, pick, precision=lax.Precision.HIGHEST, preferred_element_type=F32)
    own = n // count
    part = n // own
    for m in range(n):
        start = (m % own) * part
        o_ref[m, width:, :] = second[start : start + part, :]
    scatter_rows(ids_ref, o_ref, outs)


def mix_call(k, x, group):
    n, width, chan = x.shape
    return pl.pallas_call(
        functools.partial(mix_kernel, group),
        out_shape=jax.ShapeDtypeStruct(x.shape, F32),
        compiler_params=params(),
        cost_estimate=cost(6 * group * n * n * width * chan, 8 * n * width * chan),
        name="mix",
    )(*k, x)


SMEM_SPEC = pl.BlockSpec(memory_space=pltpu.SMEM)
VMEM_SPEC = pl.BlockSpec(memory_space=pltpu.VMEM)


def mix_second_call(ids, k, u, b, group, count, scale):
    n, width, chan = u.shape
    own = n // count
    size = n * group
    tall = width + n // own
    return pl.pallas_call(
        functools.partial(mix_second_kernel, group, scale, count),
        in_specs=[SMEM_SPEC] + [VMEM_SPEC] * 4,
        out_specs=[VMEM_SPEC] * count,
        out_shape=[jax.ShapeDtypeStruct((own, tall, chan), F32)] * count,
        scratch_shapes=[pltpu.VMEM((n, tall, chan), F32), pltpu.VMEM((size, size), F32)],
        compiler_params=params(),
        cost_estimate=cost(12 * size * n * width * chan, 12 * n * width * chan),
        name="mix_second",
    )(ids, *k, u, b)


def finish_kernel(width, ids_ref, ahead_ref, *refs):
    del ahead_ref
    pieces, (o_ref, s_ref, sem) = refs[:-3], refs[-3:]
    copies = []
    for d, piece in enumerate(pieces):
        start = pl.multiple_of(lax.bitwise_xor(ids_ref[0], d) * width, width)
        copies.append(
            pltpu.make_async_copy(piece.at[:, :width], o_ref.at[:, pl.ds(start, width)], sem.at[d])
        )
    for c in copies:
        c.start()
    total = pieces[0][:, width:, :]
    for piece in pieces[1:]:
        total = total + piece[:, width:, :]
    s_ref[...] = total
    for c in copies:
        c.wait()


def finish_call(ids, pieces, width, ahead):
    own, tall, chan = pieces[0].shape
    count = len(pieces)
    return pl.pallas_call(
        functools.partial(finish_kernel, width),
        in_specs=[SMEM_SPEC, pl.BlockSpec(memory_space=pl.ANY)] + [VMEM_SPEC] * count,
        out_specs=[pl.BlockSpec(memory_space=pltpu.HBM), VMEM_SPEC],
        out_shape=[
            pltpu.HBM((own, count * width, chan), F32),
            jax.ShapeDtypeStruct((own, tall - width, chan), F32),
        ],
        scratch_shapes=[pltpu.SemaphoreType.DMA((count,))],
        compiler_params=params(),
        cost_estimate=cost(0, 8 * own * tall * count * chan),
        name="finish",
    )(ids, ahead, *pieces)


def place_copies(offsets, ids_ref, pieces, whole, sem):
    half = pieces[0].shape[1]
    copies = []
    for piece, rels in zip(pieces, offsets):
        for u, (rel, side, flip) in enumerate(rels):
            place = 2 * lax.bitwise_xor(ids_ref[0], rel) + lax.bitwise_xor(ids_ref[1], side)
            place = 2 * place + lax.bitwise_xor(ids_ref[2], flip)
            start = pl.multiple_of(place * half, half)
            copies.append(pltpu.make_async_copy(piece.at[u], whole.at[pl.ds(start, half)], sem.at[len(copies)]))
    return copies


def up_kernel(offsets, ids_ref, g_ref, *refs):
    pieces = refs[: len(offsets)]
    o_ref, whole, g, o, sem, g_sem, o_sem = refs[len(offsets) :]
    loads = place_copies(offsets, ids_ref, pieces, whole, sem)
    g_load = pltpu.make_async_copy(g_ref, g, g_sem)
    g_load.start()
    for c in loads:
        c.start()
    g_load.wait()
    blocks, rows, chan = g.shape
    slices, _, width, _ = o.shape
    both = split(jnp.concatenate([g[m] for m in range(blocks)], axis=1))
    for c in loads:
        c.wait()
    tile = max(width, 256)
    per = tile // width
    stores = []
    for n in range(rows // tile):
        res = dot3(split(whole[:, n * tile : (n + 1) * tile]), both, TN)
        for t in range(per):
            for m in range(blocks):
                o[n * per + t, m] = res[t * width : (t + 1) * width, m * chan : (m + 1) * chan]
        part = pl.ds(n * per, per)
        stores.append(pltpu.make_async_copy(o.at[part], o_ref.at[part], o_sem.at[n]))
        stores[-1].start()
    for c in stores:
        c.wait()


def up_call(ids, pieces, offsets, grad, slices, columns):
    blocks, rows, chan = grad.shape
    shape = (slices, blocks, rows // slices, chan)
    space = pl.BlockSpec(memory_space=pltpu.HBM)
    return pl.pallas_call(
        functools.partial(up_kernel, offsets),
        in_specs=[pl.BlockSpec(memory_space=pltpu.SMEM)] + [space] * (1 + len(pieces)),
        out_specs=space,
        out_shape=pltpu.HBM(shape, F32),
        scratch_shapes=[
            pltpu.VMEM((rows, columns), F32),
            pltpu.VMEM(grad.shape, F32),
            pltpu.VMEM(shape, F32),
            pltpu.SemaphoreType.DMA((sum(map(len, offsets)),)),
            pltpu.SemaphoreType.DMA,
            pltpu.SemaphoreType.DMA((rows // 256,)),
        ],
        compiler_params=params(),
        cost_estimate=cost(6 * rows * rows * blocks * chan, 4 * rows * rows + 8 * rows * blocks * chan),
        name="up",
    )(ids, hbm(grad), *map(hbm, pieces))


def mixed_kernel(offsets, ids_ref, v_ref, f_ref, *refs):
    pieces = refs[: len(offsets)]
    o_ref, whole, v, f, o, sem, v_sem, o_sem = refs[len(offsets) :]
    loads = place_copies(offsets, ids_ref, pieces, whole, sem)
    v_loads = [
        pltpu.make_async_copy(v_ref, v, v_sem.at[0]),
        pltpu.make_async_copy(f_ref, f, v_sem.at[1]),
    ]
    for c in v_loads + loads:
        c.start()
    for c in v_loads:
        c.wait()
    slices, blocks, _, chan = v.shape
    both = split(
        jnp.concatenate(
            [jnp.concatenate([v[t, m] for m in range(blocks)], axis=1) for t in range(slices)], axis=0
        )
    )
    for c in loads:
        c.wait()
    rows = whole.shape[0]
    tile = 256
    stores = []
    for n in range(rows // tile):
        part = pl.ds(n * tile, tile)
        res = dot3(split(whole[part, :]), both, NN)
        for m in range(blocks):
            o[m, part, :] = res[:, m * chan : (m + 1) * chan] * f[m, part, :]
        stores.append(pltpu.make_async_copy(o.at[:, part], o_ref.at[:, part], o_sem.at[n]))
        stores[-1].start()
    for c in stores:
        c.wait()


def mixed_call(ids, pieces, offsets, v, factor, columns):
    blocks, rows, chan = factor.shape
    space = pl.BlockSpec(memory_space=pltpu.HBM)
    return pl.pallas_call(
        functools.partial(mixed_kernel, offsets),
        in_specs=[pl.BlockSpec(memory_space=pltpu.SMEM), pl.BlockSpec(memory_space=pl.ANY)]
        + [space] * (1 + len(pieces)),
        out_specs=space,
        out_shape=pltpu.HBM(factor.shape, F32),
        scratch_shapes=[
            pltpu.VMEM((rows, columns), F32),
            pltpu.VMEM(v.shape, F32),
            pltpu.VMEM(factor.shape, F32),
            pltpu.VMEM(factor.shape, F32),
            pltpu.SemaphoreType.DMA((sum(map(len, offsets)),)),
            pltpu.SemaphoreType.DMA((2,)),
            pltpu.SemaphoreType.DMA((rows // 256,)),
        ],
        compiler_params=params(),
        cost_estimate=cost(6 * rows * rows * blocks * chan, 4 * rows * rows + 12 * rows * blocks * chan),
        name="mixed",
    )(ids, v, hbm(factor), *map(hbm, pieces))


def flip_bits(q, bits):
    r = 0
    for b in range(bits):
        r |= ((q >> b) & 1) << (bits - 1 - b)
    return r


def first_kernel(
    bits, ids_ref, ga_hbm, gb_hbm, va_ref, vb_ref, ka_ref, sa_ref, kb_ref, sb_ref, ga_ref, gb_ref, lh, ll, sem
):
    blocks, count, unit, _ = ga_ref.shape
    loads = [
        pltpu.make_async_copy(ga_hbm, ga_ref, sem.at[0]),
        pltpu.make_async_copy(gb_hbm, gb_ref, sem.at[1]),
    ]
    for c in loads:
        c.start()
    for c in loads:
        c.wait()
    slices, _, width, _ = va_ref.shape
    for q in range(count):
        src = lax.bitwise_xor(ids_ref[0], flip_bits(q, bits))
        row = jnp.concatenate([r[m, src] for m in range(blocks) for r in (ga_ref, gb_ref)], axis=1)
        lh[q * unit : (q + 1) * unit, :], ll[q * unit : (q + 1) * unit, :] = split(row)
    left = lh[...], ll[...]
    quarter, half = count // 4, unit // 2
    tile = max(width, 256)
    per = tile // width
    for n in range(slices // per):
        v = jnp.concatenate(
            [
                jnp.concatenate([r[t, m] for m in range(blocks) for r in (va_ref, vb_ref)], axis=1)
                for t in range(n * per, (n + 1) * per)
            ],
            axis=0,
        )
        res = dot3(left, split(v), NT)
        part = slice(n * tile, (n + 1) * tile)
        for q in range(count):
            r0, r1, rest = q // (2 * quarter), (q // quarter) % 2, q % quarter
            (sa_ref if r0 else ka_ref)[r1 * quarter + rest, :, part] = res[q * unit : q * unit + half, :]
            (sb_ref if r1 else kb_ref)[r0 * quarter + rest, :, part] = res[q * unit + half : (q + 1) * unit, :]


def first_call(ids, grad_own, grad_other, v_own, v_other):
    blocks, count, unit, chan = grad_own.shape
    slices, _, width, _ = v_own.shape
    rows = slices * width
    bits = count.bit_length() - 1
    vmem = pl.BlockSpec(memory_space=pltpu.VMEM)
    shape = jax.ShapeDtypeStruct((count // 2, unit // 2, rows), F32)
    depth = 2 * blocks * chan
    return pl.pallas_call(
        functools.partial(first_kernel, bits),
        in_specs=[pl.BlockSpec(memory_space=pltpu.SMEM)]
        + [pl.BlockSpec(memory_space=pltpu.HBM)] * 2
        + [vmem] * 2,
        out_specs=[vmem] * 4,
        out_shape=[shape] * 4,
        scratch_shapes=[pltpu.VMEM(grad_own.shape, F32)] * 2
        + [pltpu.VMEM((count * unit, depth), BF16)] * 2
        + [pltpu.SemaphoreType.DMA((2,))],
        compiler_params=params(),
        cost_estimate=cost(6 * rows * count * unit * depth, 4 * (rows * count * unit + 2 * rows * depth)),
        name="first",
    )(ids, hbm(grad_own), hbm(grad_other), v_own, v_other)


def sums_kernel(ka_ref, ga_ref, kb_ref, gb_ref, oa_ref, sa_ref, ob_ref, sb_ref):
    half = oa_ref.shape[0]
    for k_ref, g_ref, o_ref, s_ref in ((ka_ref, ga_ref, oa_ref, sa_ref), (kb_ref, gb_ref, ob_ref, sb_ref)):
        s_ref[...] = k_ref[half:] + g_ref[half:]
        o_ref[...] = k_ref[:half] + g_ref[:half]


def sums_call(keep_a, got_a, keep_b, got_b):
    half, unit, columns = keep_a.shape[0] // 2, *keep_a.shape[1:]
    shape = jax.ShapeDtypeStruct((half, unit, columns), F32)
    return pl.pallas_call(
        sums_kernel,
        in_specs=[VMEM_SPEC] * 4,
        out_specs=[VMEM_SPEC] * 4,
        out_shape=[shape] * 4,
        compiler_params=params(),
        cost_estimate=cost(4 * half * unit * columns, 48 * half * unit * columns),
        name="sums",
    )(keep_a, got_a, keep_b, got_b)


def body(seq_count, rep_count, inputs, gate_in, out_grad, w_first, w_second, w_out):
    total = w_second.shape[0]
    own = total // seq_count
    rows = inputs.shape[0] // own
    chan = inputs.shape[1]
    width = rows // seq_count
    unit, columns = w_first.shape
    bits = seq_count.bit_length() - 1
    s = lax.axis_index("seq").astype(jnp.int32)
    h = lax.axis_index("chan").astype(jnp.int32)
    side = lax.rem(lax.axis_index("rep").astype(jnp.int32), 2)
    ids = jnp.stack([s, h, side])
    group = 16 if total * 16 <= 256 else 8

    def swap_core(x):
        return lax.ppermute(x, "chan", [(0, 1), (1, 0)])

    def swap_rep(x):
        return lax.ppermute(x, "rep", [(i, i ^ 1) for i in range(rep_count)])

    def swap_seq(x, bit):
        return lax.ppermute(x, "seq", [(i, i ^ bit) for i in range(seq_count)])

    def exchange(x):
        return lax.all_to_all(x, "seq", split_axis=0, concat_axis=0, tiled=True)

    def after(x, *deps):
        return lax.optimization_barrier((x, *deps))[0]

    def all_after(xs, *deps):
        return lax.optimization_barrier((*xs, *deps))[: len(xs)]

    other_cot = swap_core(out_grad)
    half = lax.dynamic_slice_in_dim(w_first, side * (unit // 2), unit // 2, 0).reshape(1, unit // 2, columns)
    far_bits = range(2, seq_count, 2)
    z_far = [swap_seq(half, b) for b in far_bits]
    z_rel = (0, *far_bits)

    own_rows = lax.dynamic_slice_in_dim(w_out, h * chan, chan, 0)
    w_cat = jnp.concatenate(
        [
            lax.dynamic_slice_in_dim(own_rows, h * chan, chan, 1),
            lax.dynamic_slice_in_dim(own_rows, (1 - h) * chan, chan, 1),
        ],
        axis=1,
    )
    grad, factor, grad_own, grad_send = gate_call(ids, out_grad, other_cot, gate_in, w_cat, own, unit)
    grad_other = swap_core(grad_send)
    mixers = spread_call(w_second, group)
    z_all = jnp.concatenate([after(half, grad, mixers[0])] + z_far, axis=0)

    sliced = inputs.reshape(own, seq_count, width, chan).transpose(1, 0, 2, 3)
    block_cols = exchange(after(sliced, z_all)).reshape(total, width, chan)

    y_all = swap_seq(z_all, 1)
    x_all = swap_rep(z_all)
    yx_all = swap_rep(y_all)
    pieces = [z_all, y_all, x_all, yx_all]
    offsets = [
        [(r, 0, 0) for r in z_rel],
        [(r ^ 1, 0, 0) for r in z_rel],
        [(r, 0, 1) for r in z_rel],
        [(r ^ 1, 0, 1) for r in z_rel],
    ]

    block_cols = after(block_cols, y_all, x_all, grad_other)
    v_cols = mix_call(mixers[:2], block_cols, group)
    v = exchange(v_cols.reshape(seq_count, own, width, chan))

    far = [swap_core(p) for p in pieces[:3]] + [swap_core(after(p, v_cols)) for p in pieces[3:]]
    offsets += [[(r, 1, f) for r, _, f in o] for o in offsets]
    pieces += far
    offsets = tuple(map(tuple, offsets))
    u = up_call(ids, pieces, offsets, grad.reshape(own, rows, chan), seq_count, columns)
    v = after(v, u)
    u_cols = exchange(u).reshape(total, width, chan)

    keep_a, send_a, keep_b, send_b = first_call(ids, grad_own, grad_other, v, swap_core(v))
    got_a, got_b = swap_seq(send_a, 1), swap_seq(send_b, 2)
    gate_grad = mixed_call(
        ids, pieces, offsets, after(v, send_a), factor.reshape(own, rows, chan), columns
    ).reshape(inputs.shape)

    in_pieces = mix_second_call(
        ids,
        mixers[2:],
        after(u_cols, gate_grad),
        block_cols,
        group,
        seq_count,
        1.0 / math.sqrt(rows * 2 * chan),
    )
    mid = seq_count // 2
    back = {0: in_pieces[0]}
    for d in range(mid, seq_count):
        back[d] = swap_seq(in_pieces[d], d)
    got_a, got_b = all_after([got_a, got_b], in_pieces[0])
    keep_a, send_a, keep_b, send_b = sums_call(keep_a, got_a, keep_b, got_b)
    got_a, got_b = swap_seq(send_a, 2), swap_seq(send_b, 1)
    for d in reversed(range(1, mid)):
        back[d] = swap_seq(after(in_pieces[d], back[mid]), d)

    got_a, got_b = all_after([got_a, got_b], *[back[d] for d in range(mid, seq_count)])
    keep = jnp.concatenate([keep_a + got_a, keep_b + got_b], axis=1)
    summed = keep
    for b in range(2, bits):
        part = keep.shape[0] // 2
        keep = keep[:part] + swap_seq(keep[part:], 1 << b)
    first_grad = keep.reshape(unit, columns) * (1.0 / math.sqrt(total * 2 * chan))

    input_grad, second = finish_call(ids, [back[d] for d in range(seq_count)], width, summed)
    input_grad = input_grad.reshape(inputs.shape)
    second = second[:, :, :total].reshape(total, total)
    second = second + swap_core(second)
    return input_grad, gate_grad, first_grad, second


def solution(mesh):
    return jax.shard_map(
        functools.partial(body, mesh.shape["seq"], mesh.shape["rep"]),
        mesh=mesh,
        in_specs=(
            P(("rep", "seq"), "chan"),
            P(("rep", "seq"), "chan"),
            P(("rep", "seq"), "chan"),
            P(("seq", "chan"), None),
            P(),
            P(),
        ),
        out_specs=(
            P(("rep", "seq"), "chan"),
            P(("rep", "seq"), "chan"),
            P(("rep", "seq", "chan"), None),
            P("rep", None),
        ),
        check_vma=False,
    )
```
